512 devices in a mesh: ctx: 32 (over z, core), head: 8 (over y, x_hi), grp: 2 (over x_lo).
Axes of the slice: x: 4 (x_hi: 2, x_lo: 2; x = x_hi * 2 + x_lo), y: 4, z: 16, core: 2. Of those that a mesh axis runs over, the one named last changes fastest.
Arguments:
- new_queries: bfloat16 [3072, 16384], P('ctx', ('head', 'grp')), may hold values from -6 to 6
- new_keys: bfloat16 [3072, 1024], P('ctx', 'head'), may hold values from -6 to 6
- new_values: bfloat16 [3072, 1024], P('ctx', 'head'), may hold values from -6 to 6
- segment_ids: int32 [3072], replicated, may hold values from 0 to 1, never falling along the last dimension, each value on 1 to 2304 neighbouring positions
- page_table: int32 [192], replicated, may hold values from 0 to 191, as said below
- decode_query_rows: bfloat16 [64, 16384], P(None, 'head'), may hold values from -6 to 6
- resident_keys: bfloat16 [64, 2048, 1024], P(None, ('ctx', 'grp'), 'head'), may hold values from -6 to 6
- resident_values: bfloat16 [64, 2048, 1024], P(None, ('ctx', 'grp'), 'head'), may hold values from -6 to 6
- res_len: int32 [64], replicated, may hold values from 1 to 2048, as said below
Outputs:
- prefill_out: bfloat16 [3072, 16384], P('ctx', ('head', 'grp'))
- paged_keys: bfloat16 [192, 16, 1024], P('ctx', None, 'head')
- paged_values: bfloat16 [192, 16, 1024], P('ctx', None, 'head')
- decode_out: bfloat16 [64, 16384], P(None, 'head')
The draws below stay inside these ranges and needn't reach their ends.
Inputs may be any that keep to these rules, and one draw needn't show every extreme that they name: The entries are a permutation of the page slots; page b lives on the ctx index b // 6 before the re-paging and on the ctx index page_table[b] // 6 after it; every ctx index receives exactly 6 pages, at most 1 from any one ctx index, and exactly 1 from some. `res_len`: some row has every resident position live and some row only one.
All inputs are finite; a program needn't handle non-finite values.
Results may differ from the reference program's by a relative error of at most 0.007.
Values may be sent and summed in bfloat16 or wider, within the bound.
No kernel may reach another device: no remote copies, remote signals or barrier semaphores. Data moves between devices by JAX's collectives and lax.ppermute only.
A program may use at most 128 MiB of HBM per device.

```python
import math
import jax
import jax.numpy as jnp
import numpy as np
from jax import lax

QUERY_HEADS = 128
KEY_VALUE_HEADS = 8
HEAD_SIZE = 128
TOKENS_PER_GROUP = 96
DECODE_ROWS = 64
NSEG = 2
PAGE_TOKENS = 16
NEW_TOKENS = 3072
PAGES_DEV = 6
NEW_TOKEN_PAGES = 192
RESIDENT_LENGTH = 2048


def draw_new_keys(key, part):
    key = jax.random.fold_in(key, 1)
    value_list = jax.random.normal(key, (NEW_TOKENS, KEY_VALUE_HEADS * HEAD_SIZE), jnp.float32)
    return jnp.clip(value_list, -6.0, 6.0).astype(jnp.bfloat16)


def draw_new_values(key, part):
    key = jax.random.fold_in(key, 4)
    block_count = NEW_TOKENS // TOKENS_PER_GROUP
    columns = KEY_VALUE_HEADS * HEAD_SIZE
    base_part = jax.random.normal(jax.random.fold_in(key, 1), (NEW_TOKENS, columns), jnp.float32)
    block_part = jax.random.normal(jax.random.fold_in(key, 2), (block_count, 1, columns), jnp.float32)
    spread_rows = jnp.broadcast_to(block_part, (block_count, TOKENS_PER_GROUP, columns)).reshape(NEW_TOKENS, columns)
    value_list = jnp.clip(0.8 * base_part + 0.6 * spread_rows, -6.0, 6.0)
    return value_list.astype(jnp.bfloat16)


def draw_new_queries(key, part):
    key = jax.random.fold_in(key, 2)
    value_list = jax.random.normal(key, (NEW_TOKENS, QUERY_HEADS * HEAD_SIZE), jnp.float32)
    return jnp.clip(value_list, -6.0, 6.0).astype(jnp.bfloat16)


def draw_decode_query_rows(key, part):
    key = jax.random.fold_in(key, 3)
    value_list = jax.random.normal(key, (DECODE_ROWS, QUERY_HEADS * HEAD_SIZE), jnp.float32)
    return jnp.clip(value_list, -6.0, 6.0).astype(jnp.bfloat16)


def draw_page_table(key, part):
    key = jax.random.fold_in(key, 7)
    ctx_total = NEW_TOKEN_PAGES // PAGES_DEV
    shuffled = jax.random.permutation(jax.random.fold_in(key, 1), ctx_total).astype(jnp.int32)
    place_ids = jnp.arange(ctx_total, dtype=jnp.int32)
    priority = jnp.where(shuffled == 1, -2, jnp.where(shuffled == ctx_total // 2, -1, place_ids))
    ordered = jnp.take(shuffled, jnp.argsort(priority))
    page_order = jax.random.permutation(jax.random.fold_in(key, 3), PAGES_DEV).astype(jnp.int32)
    local_pages = jnp.arange(PAGES_DEV, dtype=jnp.int32)
    offset_of = jnp.take(ordered, page_order % ctx_total)
    sources = jnp.arange(ctx_total, dtype=jnp.int32)[:, None]
    targets = (sources + offset_of[None, :]) % ctx_total
    slot_keys = jax.random.split(jax.random.fold_in(key, 2), ctx_total)
    slot_order = jax.vmap(lambda sub_key: jax.random.permutation(sub_key, PAGES_DEV))(slot_keys).astype(jnp.int32)
    slots = slot_order[targets, jnp.broadcast_to(local_pages[None, :], targets.shape)]
    return (targets * PAGES_DEV + slots).reshape(NEW_TOKEN_PAGES).astype(jnp.int32)


def draw_res_len(key, part):
    key = jax.random.fold_in(key, 9)
    lengths = jax.random.randint(jax.random.fold_in(key, 1), (DECODE_ROWS,), 1, RESIDENT_LENGTH + 1)
    longest = jax.random.randint(jax.random.fold_in(key, 2), (), 0, DECODE_ROWS)
    shortest = (longest + 1 + jax.random.randint(jax.random.fold_in(key, 3), (), 0, DECODE_ROWS - 1)) % DECODE_ROWS
    lengths = lengths.at[longest].set(RESIDENT_LENGTH).at[shortest].set(1)
    return lengths.astype(jnp.int32)


def block_levels(key, dims, cuts, low, largest):
    def one(axis_at, parts):
        steps = jax.random.uniform(jax.random.fold_in(jax.random.fold_in(key, 6), axis_at), (parts,), jnp.float32, low / len(cuts), largest / len(cuts))
        return jnp.repeat(jnp.exp(steps), dims[axis_at] // parts).reshape((-1,) + (1,) * (len(dims) - axis_at - 1))

    factor_of = one(*cuts[0])
    for cut in cuts[1:]:
        factor_of = factor_of * one(*cut)
    return factor_of


def profile(count, total, reach, slope):
    loads = [(1 << 20) // math.isqrt(grade ** slope) + 1 for grade in range(2, count + 1)]
    spare, counts = total - reach - (count - 1), [1] * (count - 1)
    while spare > 0:
        movable = [i for i in range(count - 1) if counts[i] < reach]
        whole, remaining = sum([loads[i] for i in movable]), spare
        for i in movable:
            addition = min(reach - counts[i], max(1, remaining * loads[i] // whole), spare)
            counts[i] = counts[i] + addition
            spare = spare - addition
    return np.array([reach] + counts)


def ragged(stream_key, amount, total, most, slope):
    if amount == 2:
        one = jax.random.randint(stream_key, (), max(1, total - most), min(most, total - 1) + 1)
        return jnp.stack([one, total - one])
    tallies = jnp.asarray(profile(amount, total, most, slope), jnp.int32)
    couples = (amount - 1) // 2
    donor, taker = tallies[1:1 + 2 * couples:2], tallies[2:2 + 2 * couples:2]
    margin = jnp.minimum(donor - 1, most - taker)
    moved = jax.random.randint(jax.random.fold_in(stream_key, 1), (couples,), 0, 1 << 20) % (margin + 1)
    tallies = tallies.at[1:1 + 2 * couples:2].set(donor - moved).at[2:2 + 2 * couples:2].set(taker + moved)
    return tallies[jax.random.permutation(jax.random.fold_in(stream_key, 2), amount)]


def bell_draw(stream_key, shape, width, limit, shards=(), kind=jnp.bfloat16):
    loudness = block_levels(stream_key, shape, shards, -0.22, 0.18) if shards else 1.0
    values = jax.random.normal(stream_key, shape, jnp.float32) * width * loudness
    return jnp.minimum(jnp.maximum(values, -limit), limit).astype(kind)


def setup_inputs(seed: int = 0) -> dict:
    key_of = jax.random.split(jax.random.key(seed), 10)
    return {
        "new_queries": draw_new_queries(jax.random.fold_in(key_of[9], 71), 0),
        "new_keys": draw_new_keys(jax.random.fold_in(key_of[9], 71), 0),
        "new_values": draw_new_values(jax.random.fold_in(key_of[9], 71), 0),
        "segment_ids": jnp.searchsorted(jnp.cumsum(ragged(key_of[3], NSEG, NEW_TOKENS, NEW_TOKENS * 3 // 4, 1)), jnp.arange(NEW_TOKENS), side="right").astype(jnp.int32),
        "page_table": draw_page_table(jax.random.fold_in(key_of[9], 71), 0),
        "decode_query_rows": draw_decode_query_rows(jax.random.fold_in(key_of[9], 71), 0),
        "resident_keys": bell_draw(key_of[6], (DECODE_ROWS, RESIDENT_LENGTH, KEY_VALUE_HEADS * HEAD_SIZE), 1.0, 6.0, ((1, 64), (2, 8))),
        "resident_values": bell_draw(key_of[7], (DECODE_ROWS, RESIDENT_LENGTH, KEY_VALUE_HEADS * HEAD_SIZE), 1.0, 6.0, ((1, 64), (2, 8))),
        "res_len": draw_res_len(jax.random.fold_in(key_of[9], 71), 0),
    }


def prefill_attention(new_queries, new_keys, new_values, segment_ids):
    repeat_factor = QUERY_HEADS // KEY_VALUE_HEADS
    score_scale = HEAD_SIZE ** -0.5
    positions = jnp.arange(NEW_TOKENS, dtype=jnp.int32)
    query_block_split = new_queries.reshape(NEW_TOKENS // TOKENS_PER_GROUP, TOKENS_PER_GROUP, KEY_VALUE_HEADS, repeat_factor, HEAD_SIZE)
    key_head_split = new_keys.reshape(NEW_TOKENS, KEY_VALUE_HEADS, HEAD_SIZE)
    value_head_split = new_values.reshape(NEW_TOKENS, KEY_VALUE_HEADS, HEAD_SIZE)
    block_starts = jnp.arange(NEW_TOKENS // TOKENS_PER_GROUP, dtype=jnp.int32) * TOKENS_PER_GROUP

    def one_block(packed):
        query_block, block_start = packed
        query_pos = block_start + jnp.arange(TOKENS_PER_GROUP, dtype=jnp.int32)
        query_seg = lax.dynamic_slice_in_dim(segment_ids, block_start.astype(jnp.int32), TOKENS_PER_GROUP)
        allowed = (positions[None, :] <= query_pos[:, None]) & (segment_ids[None, :] == query_seg[:, None])

        def heads_grouped(head_id):
            queries = jnp.take(query_block, head_id, axis=1).astype(jnp.float32)
            key_rows = jnp.take(key_head_split, head_id, axis=1).astype(jnp.float32)
            value_rows = jnp.take(value_head_split, head_id, axis=1).astype(jnp.float32)
            scores = jnp.einsum('tqd,nd->tqn', queries, key_rows) * score_scale
            scores = jnp.where(allowed[:, None, :], scores, -jnp.inf)
            top_score = jnp.max(scores, axis=-1, keepdims=True)
            weights = jnp.where(allowed[:, None, :], jnp.exp(scores - top_score), 0.0).astype(jnp.bfloat16)
            weights = weights.astype(jnp.float32)
            summed = jnp.sum(weights, axis=-1)
            weighted = jnp.einsum('tqn,nd->tqd', weights, value_rows)
            return weighted / summed[..., None]

        output_list = lax.map(heads_grouped, jnp.arange(KEY_VALUE_HEADS, dtype=jnp.int32))
        return jnp.transpose(output_list, (1, 0, 2, 3)).reshape(TOKENS_PER_GROUP, QUERY_HEADS * HEAD_SIZE)

    result = lax.map(one_block, (query_block_split, block_starts))
    return result.reshape(NEW_TOKENS, QUERY_HEADS * HEAD_SIZE).astype(jnp.bfloat16)


def decode_attention(decode_query_rows, new_keys, new_values, resident_keys, resident_values, res_len):
    repeat_factor = QUERY_HEADS // KEY_VALUE_HEADS
    score_scale = HEAD_SIZE ** -0.5
    resident_total = resident_keys.shape[1]
    query_head_split = decode_query_rows.reshape(DECODE_ROWS, KEY_VALUE_HEADS, repeat_factor, HEAD_SIZE)
    key_head_split = new_keys.reshape(NEW_TOKENS, KEY_VALUE_HEADS, HEAD_SIZE)
    value_head_split = new_values.reshape(NEW_TOKENS, KEY_VALUE_HEADS, HEAD_SIZE)
    resident_key_rows = resident_keys.reshape(DECODE_ROWS, resident_total, KEY_VALUE_HEADS, HEAD_SIZE)
    resident_value_rows = resident_values.reshape(DECODE_ROWS, resident_total, KEY_VALUE_HEADS, HEAD_SIZE)
    live = jnp.arange(resident_total, dtype=jnp.int32)[None, :] < res_len[:, None]

    def heads_grouped(head_id):
        queries = jnp.take(query_head_split, head_id, axis=1).astype(jnp.float32)
        prefix_scores = jnp.einsum('rqd,nd->rqn', queries, jnp.take(key_head_split, head_id, axis=1).astype(jnp.float32)) * score_scale
        res_scores = jnp.einsum('rqd,rpd->rqp', queries, jnp.take(resident_key_rows, head_id, axis=2).astype(jnp.float32)) * score_scale
        res_scores = jnp.where(live[:, None, :], res_scores, -jnp.inf)
        top_score = jnp.maximum(jnp.max(prefix_scores, axis=-1), jnp.max(res_scores, axis=-1))[..., None]
        prefix_weights = jnp.exp(prefix_scores - top_score).astype(jnp.bfloat16).astype(jnp.float32)
        res_weights = jnp.where(live[:, None, :], jnp.exp(res_scores - top_score), 0.0).astype(jnp.bfloat16).astype(jnp.float32)
        summed = jnp.sum(prefix_weights, axis=-1) + jnp.sum(res_weights, axis=-1)
        weighted = jnp.einsum('rqn,nd->rqd', prefix_weights, jnp.take(value_head_split, head_id, axis=1).astype(jnp.float32))
        weighted = weighted + jnp.einsum('rqp,rpd->rqd', res_weights, jnp.take(resident_value_rows, head_id, axis=2).astype(jnp.float32))
        return weighted / summed[..., None]

    output_list = lax.map(heads_grouped, jnp.arange(KEY_VALUE_HEADS, dtype=jnp.int32))
    return jnp.transpose(output_list, (1, 0, 2, 3)).reshape(DECODE_ROWS, QUERY_HEADS * HEAD_SIZE).astype(jnp.bfloat16)


def reference(new_queries, new_keys, new_values, segment_ids, page_table, decode_query_rows, resident_keys, resident_values, res_len):
    prefill_out = prefill_attention(new_queries, new_keys, new_values, segment_ids)
    key_page_split = new_keys.reshape(NEW_TOKEN_PAGES, PAGE_TOKENS, KEY_VALUE_HEADS * HEAD_SIZE)
    value_page_split = new_values.reshape(NEW_TOKEN_PAGES, PAGE_TOKENS, KEY_VALUE_HEADS * HEAD_SIZE)
    paged_keys = jnp.zeros_like(key_page_split).at[page_table].set(key_page_split)
    paged_values = jnp.zeros_like(value_page_split).at[page_table].set(value_page_split)
    decode_out = decode_attention(decode_query_rows, new_keys, new_values, resident_keys, resident_values, res_len)
    return prefill_out, paged_keys, paged_values, decode_out
```

```python
import jax
import jax.numpy as jnp
import numpy as np
from jax import lax
from jax.experimental import pallas as pl
from jax.experimental.pallas import tpu as pltpu
from jax.sharding import Mesh, PartitionSpec as P

HEAD_SIZE = 128
PAGE_TOKENS = 16
NEG_FILL = -1e30
LOG2_SCALE = HEAD_SIZE**-0.5 * 1.4426950408889634
VMEM = pl.BlockSpec(memory_space=pltpu.VMEM)
SMEM = pl.BlockSpec(memory_space=pltpu.SMEM)
PARAMS = pltpu.CompilerParams(vmem_limit_bytes=48 * 1024 * 1024)


def dot_t(a, b):
    return lax.dot_general(a, b, (((1,), (1,)), ((), ())), preferred_element_type=jnp.float32)


def dot(a, b):
    return jnp.dot(a, b, preferred_element_type=jnp.float32)


def as_rows(column):
    eye = lax.broadcasted_iota(jnp.int32, (128, 128), 0) == lax.broadcasted_iota(
        jnp.int32, (128, 128), 1
    )
    return [
        jnp.sum(jnp.where(eye, column[i : i + 128], 0.0), axis=0, keepdims=True) for i in (0, 128)
    ]


def stat_rows(top, total):
    high = total.astype(jnp.bfloat16).astype(jnp.float32)
    rows = [top, high, total - high, jnp.zeros((10, 128), jnp.float32)]
    return jnp.concatenate(rows, axis=0).astype(jnp.bfloat16)


def partial_kernel(len_ref, where_ref, dq_ref, rk_ref, rv_ref, nk_ref, nv_ref, out_ref):
    groups = out_ref.shape[0]
    res_rows = rk_ref.shape[1]
    heads = dq_ref.shape[1] // HEAD_SIZE
    tokens = nk_ref.shape[0]
    base, grp, half_rows = where_ref[0], where_ref[1], where_ref[2]
    keys = 16 * res_rows
    queries = 16 * heads
    col = lax.broadcasted_iota(jnp.int32, (1, keys), 1)
    col_row = col // res_rows
    col_pos = base + col % res_rows
    same_row = (lax.broadcasted_iota(jnp.int32, (queries, keys), 0) % 16) == (
        lax.broadcasted_iota(jnp.int32, (queries, keys), 1) // res_rows
    )
    token = lax.broadcasted_iota(jnp.int32, (1, tokens), 1) - grp * half_rows
    token_bias = jnp.where((token >= 0) & (token < half_rows), 0.0, NEG_FILL)
    nk = nk_ref[...]
    nv = nv_ref[...]
    for g in range(groups):
        lens = jnp.zeros((1, keys), jnp.int32)
        for r in range(16):
            lens = jnp.where(col_row == r, len_ref[16 * g + r], lens)
        live = jnp.where(col_pos < lens, 0.0, NEG_FILL)
        q = jnp.concatenate(
            [
                dq_ref[16 * g : 16 * g + 16, h * HEAD_SIZE : (h + 1) * HEAD_SIZE]
                for h in range(heads)
            ],
            axis=0,
        )
        rk = rk_ref[16 * g : 16 * g + 16].reshape(keys, HEAD_SIZE)
        rv = rv_ref[16 * g : 16 * g + 16].reshape(keys, HEAD_SIZE)
        s1 = jnp.where(same_row, dot_t(q, rk) * LOG2_SCALE + live, NEG_FILL)
        s2 = dot_t(q, nk) * LOG2_SCALE + token_bias
        top = jnp.maximum(
            jnp.max(s1, axis=1, keepdims=True), jnp.max(s2, axis=1, keepdims=True)
        )
        top = top.astype(jnp.bfloat16).astype(jnp.float32)
        p1 = jnp.exp2(s1 - top).astype(jnp.bfloat16)
        p2 = jnp.exp2(s2 - top).astype(jnp.bfloat16)
        total = jnp.sum(p1.astype(jnp.float32), axis=1, keepdims=True) + jnp.sum(
            p2.astype(jnp.float32), axis=1, keepdims=True
        )
        out_ref[g, :queries] = (dot(p1, rv) + dot(p2, nv)).astype(jnp.bfloat16)
        out_ref[g, queries : queries + 16] = stat_rows(
            jnp.concatenate(as_rows(top), axis=0), jnp.concatenate(as_rows(total), axis=0)
        )


def joined(parts, begin, queries, normal):
    count = parts.shape[0]
    stats = [
        parts[d, begin + queries : begin + queries + 16].astype(jnp.float32) for d in range(count)
    ]
    top = stats[0][0:2]
    for d in range(1, count):
        top = jnp.maximum(top, stats[d][0:2])
    factors = [jnp.exp2(stats[d][0:2] - top) for d in range(count)]
    total = factors[0] * (stats[0][2:4] + stats[0][4:6])
    for d in range(1, count):
        total = total + factors[d] * (stats[d][2:4] + stats[d][4:6])
    if normal:
        factors = [f / total for f in factors]
    columns = jnp.concatenate(factors, axis=0).T
    halves = []
    for half in range(2):
        rows = slice(begin + 128 * half, begin + 128 * half + 128)
        acc = jnp.zeros((128, HEAD_SIZE), jnp.float32)
        for d in range(count):
            acc = acc + parts[d, rows].astype(jnp.float32) * columns[:, 2 * d + half : 2 * d + half + 1]
        halves.append(acc)
    return halves, top, total


def pack_kernel(part_ref, nk_ref, nv_ref, out_ref):
    tokens = nk_ref.shape[0]
    queries = part_ref.shape[1] - 16
    halves, top, total = joined(part_ref, 0, queries, False)
    begin = 2 * tokens
    out_ref[:tokens] = nk_ref[...]
    out_ref[tokens:begin] = nv_ref[...]
    for half in range(2):
        out_ref[begin + 128 * half : begin + 128 * half + 128] = halves[half].astype(jnp.bfloat16)
    out_ref[begin + queries : begin + queries + 16] = stat_rows(top, total)


def decoded_kernel(tokens, all_ref, kv_ref, dec_ref):
    count = all_ref.shape[0]
    begin = 2 * tokens
    queries = all_ref.shape[1] - begin - 16
    for d in range(count):
        kv_ref[d * begin : (d + 1) * begin] = all_ref[d, :begin]
    halves, _, _ = joined(all_ref, begin, queries, True)
    for half in range(2):
        value = halves[half].astype(jnp.bfloat16)
        dec_ref[128 * half : 128 * half + 128] = value
        kv_ref[count * begin + 128 * half : count * begin + 128 * half + 128] = value


def prefill_kernel(
    where_ref, page_ref, q_ref, own_ref, peer_ref, out_ref, pk_ref, pv_ref, qs, acc, top
):
    ctx, core, bound = where_ref[0], where_ref[1], where_ref[2]
    tokens = q_ref.shape[0]
    heads = q_ref.shape[1] // HEAD_SIZE
    blocks_per = 2
    block = 2 * blocks_per * tokens
    row_block = 2 * tokens
    for s in range(pk_ref.shape[0]):
        source = page_ref[s] // (tokens // PAGE_TOKENS)
        row = pl.multiple_of(
            (source // 2) * (2 * tokens)
            + (page_ref[s] - source * (tokens // PAGE_TOKENS)) * PAGE_TOKENS,
            PAGE_TOKENS,
        )
        value_row = pl.multiple_of(row + tokens, PAGE_TOKENS)
        is_own = source % 2 == core

        @pl.when(is_own)
        def _():
            pk_ref[s] = own_ref[pl.ds(row, PAGE_TOKENS), :]
            pv_ref[s] = own_ref[pl.ds(value_row, PAGE_TOKENS), :]

        @pl.when(jnp.logical_not(is_own))
        def _():
            pk_ref[s] = peer_ref[pl.ds(row, PAGE_TOKENS), :]
            pv_ref[s] = peer_ref[pl.ds(value_row, PAGE_TOKENS), :]

    for h in range(heads):
        qs[h * tokens : (h + 1) * tokens] = q_ref[:, h * HEAD_SIZE : (h + 1) * HEAD_SIZE]
    acc[...] = jnp.zeros_like(acc)
    top[...] = jnp.full_like(top, NEG_FILL)
    first = ctx * tokens
    q_pos = first + lax.broadcasted_iota(jnp.int32, (row_block, 1), 0) % tokens
    begin = jnp.where(q_pos < bound, 0, bound)
    col = lax.broadcasted_iota(jnp.int32, (1, block), 1)
    piece = col // tokens
    side = jnp.where(piece < blocks_per, core, 1 - core)
    key_pos0 = (2 * (piece % blocks_per) + side) * tokens + col % tokens
    ones = jnp.ones((block, HEAD_SIZE), jnp.bfloat16)
    lowest = jnp.where(first < bound, 0, bound) // block
    highest = first // block + 1

    def one(step, carry):
        rows = [
            pl.multiple_of((step * blocks_per + i) * 2 * tokens, PAGE_TOKENS)
            for i in range(blocks_per)
        ]
        k = jnp.concatenate(
            [ref[pl.ds(r, tokens), :] for ref in (own_ref, peer_ref) for r in rows], axis=0
        )
        v = jnp.concatenate(
            [
                ref[pl.ds(pl.multiple_of(r + tokens, PAGE_TOKENS), tokens), :]
                for ref in (own_ref, peer_ref)
                for r in rows
            ],
            axis=0,
        )
        v = jnp.concatenate([v, ones], axis=1)
        key_pos = key_pos0 + step * block
        bias = jnp.where((key_pos <= q_pos) & (key_pos >= begin), 0.0, NEG_FILL)
        for b in range(heads * tokens // row_block):
            rows_b = slice(b * row_block, (b + 1) * row_block)
            s = dot_t(qs[rows_b], k) * LOG2_SCALE + bias
            before = top[rows_b]
            after = jnp.maximum(before, jnp.max(s, axis=1, keepdims=True))
            p = jnp.exp2(s - after).astype(jnp.bfloat16)
            acc[rows_b] = acc[rows_b] * jnp.exp2(before - after) + dot(p, v)
            top[rows_b] = after
        return carry

    lax.fori_loop(lowest, highest, one, 0)
    for h in range(heads):
        rows_h = slice(h * tokens, (h + 1) * tokens)
        out_ref[:, h * HEAD_SIZE : (h + 1) * HEAD_SIZE] = (
            acc[rows_h, :HEAD_SIZE] / acc[rows_h, HEAD_SIZE:]
        ).astype(jnp.bfloat16)


def place_kernel(where_ref, own_ref, core_ref, grp_ref, both_ref, out_ref):
    me = where_ref[3]
    for flip, ref in ((0, own_ref), (2, core_ref), (1, grp_ref), (3, both_ref)):
        target = me + flip - 2 * (me & flip)
        row = pl.multiple_of(target * 16, 16)
        begin = ref.shape[0] - 16 * (out_ref.shape[1] // HEAD_SIZE)
        for h in range(out_ref.shape[1] // HEAD_SIZE):
            out_ref[pl.ds(row, 16), h * HEAD_SIZE : (h + 1) * HEAD_SIZE] = ref[
                begin + 16 * h : begin + 16 * h + 16
            ]


def local(
    new_queries,
    new_keys,
    new_values,
    segment_ids,
    page_table,
    decode_query_rows,
    resident_keys,
    resident_values,
    res_len,
):
    bf = jnp.bfloat16
    tokens = new_keys.shape[0]
    ring = lax.axis_size("z")
    z, core, grp = (lax.axis_index(a) for a in ("z", "core", "grp"))
    ctx = z * 2 + core
    rows, width = decode_query_rows.shape
    queries = 16 * (width // HEAD_SIZE)
    res_rows = resident_keys.shape[1]
    pages = tokens // PAGE_TOKENS
    i32 = jnp.int32

    where_a = jnp.stack([(ctx * 2 + grp) * res_rows, grp, jnp.int32(tokens // 2)]).astype(i32)
    part = pl.pallas_call(
        partial_kernel,
        out_shape=jax.ShapeDtypeStruct((rows // 16, queries + 16, HEAD_SIZE), bf),
        in_specs=[SMEM, SMEM] + [VMEM] * 5,
        out_specs=VMEM,
        compiler_params=PARAMS,
    )(res_len, where_a, decode_query_rows, resident_keys, resident_values, new_keys, new_values)
    part = lax.all_to_all(part, ("core", "grp"), 0, 0, tiled=True)

    packed = pl.pallas_call(
        pack_kernel,
        out_shape=jax.ShapeDtypeStruct((2 * tokens + queries + 16, HEAD_SIZE), bf),
        in_specs=[VMEM] * 3,
        out_specs=VMEM,
        compiler_params=PARAMS,
    )(part, new_keys, new_values)
    gathered = lax.all_gather(packed, "z", axis=0)

    kv, dec = pl.pallas_call(
        lambda *refs: decoded_kernel(tokens, *refs),
        out_shape=(
            jax.ShapeDtypeStruct((ring * 2 * tokens + queries, HEAD_SIZE), bf),
            jax.ShapeDtypeStruct((queries, HEAD_SIZE), bf),
        ),
        in_specs=[VMEM],
        out_specs=(VMEM, VMEM),
        compiler_params=PARAMS,
    )(gathered)
    swap = [(0, 1), (1, 0)]
    peer_kv = lax.ppermute(kv, "core", swap)
    grp_dec = lax.ppermute(dec, "grp", swap)
    both_dec = lax.ppermute(grp_dec, "core", swap)

    bound = jnp.sum((segment_ids == 0).astype(i32))
    slots = ctx * pages + jnp.arange(pages, dtype=i32)
    ids = jnp.arange(page_table.shape[0], dtype=i32)
    page_from = jnp.sum(jnp.where(page_table[None, :] == slots[:, None], ids[None, :], 0), axis=1)
    where_b = jnp.stack([ctx, core, bound, core * 2 + grp]).astype(i32)
    prefill_out, paged_keys, paged_values = pl.pallas_call(
        prefill_kernel,
        out_shape=(
            jax.ShapeDtypeStruct(new_queries.shape, bf),
            jax.ShapeDtypeStruct((pages, PAGE_TOKENS, HEAD_SIZE), bf),
            jax.ShapeDtypeStruct((pages, PAGE_TOKENS, HEAD_SIZE), bf),
        ),
        in_specs=[SMEM, SMEM] + [VMEM] * 3,
        out_specs=(VMEM,) * 3,
        scratch_shapes=[
            pltpu.VMEM((tokens * (new_queries.shape[1] // HEAD_SIZE), HEAD_SIZE), bf),
            pltpu.VMEM(
                (tokens * (new_queries.shape[1] // HEAD_SIZE), 2 * HEAD_SIZE), jnp.float32
            ),
            pltpu.VMEM((tokens * (new_queries.shape[1] // HEAD_SIZE), 1), jnp.float32),
        ],
        compiler_params=PARAMS,
    )(where_b, page_from, new_queries, kv, peer_kv)

    decode_out = pl.pallas_call(
        place_kernel,
        out_shape=jax.ShapeDtypeStruct((rows, width), bf),
        in_specs=[SMEM] + [VMEM] * 4,
        out_specs=VMEM,
        compiler_params=PARAMS,
    )(where_b, dec, peer_kv, grp_dec, both_dec)
    return (prefill_out, paged_keys, paged_values, decode_out)


def solution(mesh):
    sizes = mesh.shape
    fine = Mesh(
        np.asarray(mesh.devices).reshape(sizes["ctx"] // 2, 2, sizes["head"], sizes["grp"]),
        ("z", "core", "head", "grp"),
    )
    ctx = ("z", "core")
    return jax.shard_map(
        local,
        mesh=fine,
        in_specs=(
            P(ctx, ("head", "grp")),
            P(ctx, "head"),
            P(ctx, "head"),
            P(),
            P(),
            P(None, "head"),
            P(None, ("z", "core", "grp"), "head"),
            P(None, ("z", "core", "grp"), "head"),
            P(),
        ),
        out_specs=(
            P(ctx, ("head", "grp")),
            P(ctx, None, "head"),
            P(ctx, None, "head"),
            P(None, "head"),
        ),
        check_vma=False,
    )
```

```python
import jax
import jax.numpy as jnp
import numpy as np
from jax import lax
from jax.experimental import pallas as pl
from jax.experimental.pallas import tpu as pltpu
from jax.sharding import Mesh, PartitionSpec as P

HEAD_SIZE = 128
PAGE_TOKENS = 16
NEG_FILL = -1e30
LOG2_SCALE = HEAD_SIZE**-0.5 * 1.4426950408889634
VMEM = pl.BlockSpec(memory_space=pltpu.VMEM)
SMEM = pl.BlockSpec(memory_space=pltpu.SMEM)
PARAMS = pltpu.CompilerParams(vmem_limit_bytes=48 * 1024 * 1024)


def dot_t(a, b):
    return lax.dot_general(a, b, (((1,), (1,)), ((), ())), preferred_element_type=jnp.float32)


def dot(a, b):
    return jnp.dot(a, b, preferred_element_type=jnp.float32)


def as_rows(column):
    eye = lax.broadcasted_iota(jnp.int32, (128, 128), 0) == lax.broadcasted_iota(
        jnp.int32, (128, 128), 1
    )
    return [
        jnp.sum(jnp.where(eye, column[i : i + 128], 0.0), axis=0, keepdims=True) for i in (0, 128)
    ]


def partial_kernel(len_ref, where_ref, dq_ref, rk_ref, rv_ref, nk_ref, nv_ref, out_ref):
    g = pl.program_id(0)
    res_rows = rk_ref.shape[1]
    heads = dq_ref.shape[1] // HEAD_SIZE
    tokens = nk_ref.shape[0]
    base, grp, half_rows = where_ref[0], where_ref[1], where_ref[2]
    keys = 16 * res_rows
    queries = 16 * heads
    col = lax.broadcasted_iota(jnp.int32, (1, keys), 1)
    col_row = col // res_rows
    col_pos = base + col % res_rows
    same_row = (lax.broadcasted_iota(jnp.int32, (queries, keys), 0) % 16) == (
        lax.broadcasted_iota(jnp.int32, (queries, keys), 1) // res_rows
    )
    token = lax.broadcasted_iota(jnp.int32, (1, tokens), 1) - grp * half_rows
    token_bias = jnp.where((token >= 0) & (token < half_rows), 0.0, NEG_FILL)
    lens = jnp.zeros((1, keys), jnp.int32)
    for r in range(16):
        lens = jnp.where(col_row == r, len_ref[16 * g + r], lens)
    live = jnp.where(col_pos < lens, 0.0, NEG_FILL)
    q = jnp.concatenate(
        [dq_ref[:, h * HEAD_SIZE : (h + 1) * HEAD_SIZE] for h in range(heads)], axis=0
    )
    rk = rk_ref[...].reshape(keys, HEAD_SIZE)
    rv = rv_ref[...].reshape(keys, HEAD_SIZE)
    s1 = jnp.where(same_row, dot_t(q, rk) * LOG2_SCALE + live, NEG_FILL)
    s2 = dot_t(q, nk_ref[...]) * LOG2_SCALE + token_bias
    top = jnp.maximum(jnp.max(s1, axis=1, keepdims=True), jnp.max(s2, axis=1, keepdims=True))
    top = top.astype(jnp.bfloat16).astype(jnp.float32)
    p1 = jnp.exp2(s1 - top).astype(jnp.bfloat16)
    p2 = jnp.exp2(s2 - top).astype(jnp.bfloat16)
    total = jnp.sum(p1.astype(jnp.float32), axis=1, keepdims=True) + jnp.sum(
        p2.astype(jnp.float32), axis=1, keepdims=True
    )
    out_ref[0, :queries] = (dot(p1, rv) + dot(p2, nv_ref[...])).astype(jnp.bfloat16)
    high = total.astype(jnp.bfloat16).astype(jnp.float32)
    stats = as_rows(top) + as_rows(high) + as_rows(total - high)
    stats = jnp.concatenate(stats + [jnp.zeros((10, 128), jnp.float32)], axis=0)
    out_ref[0, queries : queries + 16] = stats.astype(jnp.bfloat16)


def pack_kernel(part_ref, out_ref):
    count = part_ref.shape[0]
    queries = part_ref.shape[1] - 16
    ring, rows = out_ref.shape[0], out_ref.shape[1] // 2
    stats = [part_ref[d, queries : queries + 16].astype(jnp.float32) for d in range(count)]
    top = stats[0][0:2]
    for d in range(1, count):
        top = jnp.maximum(top, stats[d][0:2])
    factors = [jnp.exp2(stats[d][0:2] - top) for d in range(count)]
    total = factors[0] * (stats[0][2:4] + stats[0][4:6])
    for d in range(1, count):
        total = total + factors[d] * (stats[d][2:4] + stats[d][4:6])
    high = total.astype(jnp.bfloat16).astype(jnp.float32)
    columns = factors + [top, high, total - high, jnp.zeros((2, 128), jnp.float32)]
    columns = jnp.concatenate(columns, axis=0).T
    lane = lax.broadcasted_iota(jnp.int32, (128, 128), 1)
    for half in range(2):
        acc = jnp.zeros((128, HEAD_SIZE), jnp.float32)
        for d in range(count):
            part = part_ref[d, 128 * half : 128 * half + 128].astype(jnp.float32)
            acc = acc + part * columns[:, 2 * d + half : 2 * d + half + 1]
        side = jnp.zeros((128, 128), jnp.float32)
        for i in range(3):
            at = 2 * (count + i) + half
            side = jnp.where(lane == i, columns[:, at : at + 1], side)
        out_ref[half * ring // 2 : (half + 1) * ring // 2, :rows] = acc.astype(
            jnp.bfloat16
        ).reshape(ring // 2, rows, HEAD_SIZE)
        out_ref[half * ring // 2 : (half + 1) * ring // 2, rows:] = side.astype(
            jnp.bfloat16
        ).reshape(ring // 2, rows, HEAD_SIZE)


def finish_kernel(part_ref, nk_ref, nv_ref, out_ref):
    tokens = nk_ref.shape[0]
    count = part_ref.shape[0]
    rows = part_ref.shape[1] // 2
    stats = [part_ref[d, rows:].astype(jnp.float32) for d in range(count)]
    top = stats[0][:, 0:1]
    for d in range(1, count):
        top = jnp.maximum(top, stats[d][:, 0:1])
    total = jnp.zeros((rows, 1), jnp.float32)
    acc = jnp.zeros((rows, HEAD_SIZE), jnp.float32)
    for d in range(count):
        factor = jnp.exp2(stats[d][:, 0:1] - top)
        total = total + factor * (stats[d][:, 1:2] + stats[d][:, 2:3])
        acc = acc + factor * part_ref[d, :rows].astype(jnp.float32)
    out_ref[:tokens] = nk_ref[...]
    out_ref[tokens : 2 * tokens] = nv_ref[...]
    out_ref[2 * tokens :] = (acc / total).astype(jnp.bfloat16)


def spread_kernel(tokens, all_ref, out_ref):
    rows = all_ref.shape[1] - 2 * tokens
    for d in range(out_ref.shape[0]):
        for i in range(all_ref.shape[0]):
            out_ref[d, rows * i : rows * (i + 1)] = all_ref[i, 2 * tokens :]


def prefill_kernel(
    where_ref, page_ref, q_ref, own_ref, peer_ref, out_ref, pk_ref, pv_ref, qs, acc, top
):
    ctx, core, bound = where_ref[0], where_ref[1], where_ref[2]
    tokens = q_ref.shape[0]
    heads = q_ref.shape[1] // HEAD_SIZE
    blocks_per = 2
    block = 2 * blocks_per * tokens
    row_block = 2 * tokens
    for s in range(pk_ref.shape[0]):
        source = page_ref[s] // (tokens // PAGE_TOKENS)
        z = source // 2
        row = (page_ref[s] - source * (tokens // PAGE_TOKENS)) * PAGE_TOKENS
        row = pl.multiple_of(row, PAGE_TOKENS)
        value_row = pl.multiple_of(row + tokens, PAGE_TOKENS)
        is_own = source % 2 == core

        @pl.when(is_own)
        def _():
            pk_ref[s] = own_ref[z, pl.ds(row, PAGE_TOKENS), :]
            pv_ref[s] = own_ref[z, pl.ds(value_row, PAGE_TOKENS), :]

        @pl.when(jnp.logical_not(is_own))
        def _():
            pk_ref[s] = peer_ref[z, pl.ds(row, PAGE_TOKENS), :]
            pv_ref[s] = peer_ref[z, pl.ds(value_row, PAGE_TOKENS), :]

    for h in range(heads):
        qs[h * tokens : (h + 1) * tokens] = q_ref[:, h * HEAD_SIZE : (h + 1) * HEAD_SIZE]
    acc[...] = jnp.zeros_like(acc)
    top[...] = jnp.full_like(top, NEG_FILL)
    first = ctx * tokens
    q_pos = first + lax.broadcasted_iota(jnp.int32, (row_block, 1), 0) % tokens
    begin = jnp.where(q_pos < bound, 0, bound)
    col = lax.broadcasted_iota(jnp.int32, (1, block), 1)
    piece = col // tokens
    side = jnp.where(piece < blocks_per, core, 1 - core)
    key_pos0 = (2 * (piece % blocks_per) + side) * tokens + col % tokens
    ones = jnp.ones((block, HEAD_SIZE), jnp.bfloat16)
    lowest = jnp.where(first < bound, 0, bound) // block
    highest = first // block + 1

    def one(step, carry):
        pairs = [(ref, step * blocks_per + i) for ref in (own_ref, peer_ref) for i in range(blocks_per)]
        k = jnp.concatenate([ref[z, :tokens] for ref, z in pairs], axis=0)
        v = jnp.concatenate([ref[z, tokens : 2 * tokens] for ref, z in pairs], axis=0)
        v = jnp.concatenate([v, ones], axis=1)
        key_pos = key_pos0 + step * block
        bias = jnp.where((key_pos <= q_pos) & (key_pos >= begin), 0.0, NEG_FILL)
        for b in range(heads * tokens // row_block):
            rows_b = slice(b * row_block, (b + 1) * row_block)
            s = dot_t(qs[rows_b], k) * LOG2_SCALE + bias
            before = top[rows_b]
            after = jnp.maximum(before, jnp.max(s, axis=1, keepdims=True))
            p = jnp.exp2(s - after).astype(jnp.bfloat16)
            acc[rows_b] = acc[rows_b] * jnp.exp2(before - after) + dot(p, v)
            top[rows_b] = after
        return carry

    lax.fori_loop(lowest, highest, one, 0)
    for h in range(heads):
        rows_h = slice(h * tokens, (h + 1) * tokens)
        out_ref[:, h * HEAD_SIZE : (h + 1) * HEAD_SIZE] = (
            acc[rows_h, :HEAD_SIZE] / acc[rows_h, HEAD_SIZE:]
        ).astype(jnp.bfloat16)


def place_kernel(in_ref, out_ref):
    for g in range(in_ref.shape[0]):
        for h in range(out_ref.shape[1] // HEAD_SIZE):
            out_ref[16 * g : 16 * g + 16, h * HEAD_SIZE : (h + 1) * HEAD_SIZE] = in_ref[
                g, 16 * h : 16 * h + 16
            ]


def local(
    new_queries,
    new_keys,
    new_values,
    segment_ids,
    page_table,
    decode_query_rows,
    resident_keys,
    resident_values,
    res_len,
):
    bf = jnp.bfloat16
    tokens = new_keys.shape[0]
    ring = lax.axis_size("z")
    z, core, grp = (lax.axis_index(a) for a in ("z", "core", "grp"))
    ctx = z * 2 + core
    rows, width = decode_query_rows.shape
    queries = 16 * (width // HEAD_SIZE)
    res_rows = resident_keys.shape[1]
    pages = tokens // PAGE_TOKENS
    i32 = jnp.int32

    where_a = jnp.stack([(ctx * 2 + grp) * res_rows, grp, jnp.int32(tokens // 2)]).astype(i32)
    groups = rows // 16
    resident = pl.BlockSpec((16, res_rows, HEAD_SIZE), lambda g: (g, 0, 0))
    whole = pl.BlockSpec((tokens, HEAD_SIZE), lambda g: (0, 0))
    part = pl.pallas_call(
        partial_kernel,
        grid=(groups,),
        out_shape=jax.ShapeDtypeStruct((groups, queries + 16, HEAD_SIZE), bf),
        in_specs=[SMEM, SMEM, pl.BlockSpec((16, width), lambda g: (g, 0))]
        + [resident] * 2
        + [whole] * 2,
        out_specs=pl.BlockSpec((1, queries + 16, HEAD_SIZE), lambda g: (g, 0, 0)),
        compiler_params=PARAMS,
    )(res_len, where_a, decode_query_rows, resident_keys, resident_values, new_keys, new_values)
    part = lax.all_to_all(part, ("core", "grp"), 0, 0, tiled=True)
    part = pl.pallas_call(
        pack_kernel,
        out_shape=jax.ShapeDtypeStruct((ring, 2 * queries // ring, HEAD_SIZE), bf),
        in_specs=[VMEM],
        out_specs=VMEM,
        compiler_params=PARAMS,
    )(part)
    part = lax.all_to_all(part, "z", 0, 0, tiled=True)
    packed = pl.pallas_call(
        finish_kernel,
        out_shape=jax.ShapeDtypeStruct((2 * tokens + queries // ring, HEAD_SIZE), bf),
        in_specs=[VMEM] * 3,
        out_specs=VMEM,
        compiler_params=PARAMS,
    )(part, new_keys, new_values)
    kv = lax.all_gather(packed, "z", axis=0)
    peer_kv = lax.ppermute(kv, "core", [(0, 1), (1, 0)])
    dec = pl.pallas_call(
        lambda *refs: spread_kernel(tokens, *refs),
        out_shape=jax.ShapeDtypeStruct((groups, queries, HEAD_SIZE), bf),
        in_specs=[VMEM],
        out_specs=VMEM,
        compiler_params=PARAMS,
    )(kv)
    dec = lax.all_to_all(dec, ("core", "grp"), 0, 0, tiled=True)

    bound = jnp.sum((segment_ids == 0).astype(i32))
    slots = ctx * pages + jnp.arange(pages, dtype=i32)
    ids = jnp.arange(page_table.shape[0], dtype=i32)
    page_from = jnp.sum(jnp.where(page_table[None, :] == slots[:, None], ids[None, :], 0), axis=1)
    where_b = jnp.stack([ctx, core, bound]).astype(i32)
    prefill_out, paged_keys, paged_values = pl.pallas_call(
        prefill_kernel,
        out_shape=(
            jax.ShapeDtypeStruct(new_queries.shape, bf),
            jax.ShapeDtypeStruct((pages, PAGE_TOKENS, HEAD_SIZE), bf),
            jax.ShapeDtypeStruct((pages, PAGE_TOKENS, HEAD_SIZE), bf),
        ),
        in_specs=[SMEM, SMEM] + [VMEM] * 3,
        out_specs=(VMEM,) * 3,
        scratch_shapes=[
            pltpu.VMEM((tokens * (new_queries.shape[1] // HEAD_SIZE), HEAD_SIZE), bf),
            pltpu.VMEM(
                (tokens * (new_queries.shape[1] // HEAD_SIZE), 2 * HEAD_SIZE), jnp.float32
            ),
            pltpu.VMEM((tokens * (new_queries.shape[1] // HEAD_SIZE), 1), jnp.float32),
        ],
        compiler_params=PARAMS,
    )(where_b, page_from, new_queries, kv, peer_kv)

    dec = lax.optimization_barrier((dec, paged_keys))[0]
    decode_out = pl.pallas_call(
        place_kernel,
        out_shape=jax.ShapeDtypeStruct((rows, width), bf),
        in_specs=[VMEM],
        out_specs=VMEM,
        compiler_params=PARAMS,
    )(dec)
    return (prefill_out, paged_keys, paged_values, decode_out)


def solution(mesh):
    sizes = mesh.shape
    fine = Mesh(
        np.asarray(mesh.devices).reshape(sizes["ctx"] // 2, 2, sizes["head"], sizes["grp"]),
        ("z", "core", "head", "grp"),
    )
    ctx = ("z", "core")
    return jax.shard_map(
        local,
        mesh=fine,
        in_specs=(
            P(ctx, ("head", "grp")),
            P(ctx, "head"),
            P(ctx, "head"),
            P(),
            P(),
            P(None, "head"),
            P(None, ("z", "core", "grp"), "head"),
            P(None, ("z", "core", "grp"), "head"),
            P(),
        ),
        out_specs=(
            P(ctx, ("head", "grp")),
            P(ctx, None, "head"),
            P(ctx, None, "head"),
            P(None, "head"),
        ),
        check_vma=False,
    )
```

```python
import jax
import jax.numpy as jnp
import numpy as np
from jax import lax
from jax.experimental import pallas as pl
from jax.experimental.pallas import tpu as pltpu
from jax.sharding import Mesh, PartitionSpec as P

HEAD_SIZE = 128
PAGE_TOKENS = 16
NEG_FILL = -1e30
LOG2_SCALE = HEAD_SIZE**-0.5 * 1.4426950408889634
VMEM = pl.BlockSpec(memory_space=pltpu.VMEM)
HBM = pl.BlockSpec(memory_space=pltpu.HBM)
SMEM = pl.BlockSpec(memory_space=pltpu.SMEM)
PARAMS = pltpu.CompilerParams(vmem_limit_bytes=48 * 1024 * 1024)


def dot_t(a, b):
    return lax.dot_general(a, b, (((1,), (1,)), ((), ())), preferred_element_type=jnp.float32)


def dot(a, b):
    return jnp.dot(a, b, preferred_element_type=jnp.float32)


def as_rows(column):
    eye = lax.broadcasted_iota(jnp.int32, (128, 128), 0) == lax.broadcasted_iota(
        jnp.int32, (128, 128), 1
    )
    return [
        jnp.sum(jnp.where(eye, column[i : i + 128], 0.0), axis=0, keepdims=True) for i in (0, 128)
    ]


def partial_kernel(
    len_ref, where_ref, dq_hbm, rk_hbm, rv_hbm, nk_hbm, nv_hbm, out_ref, dq, rk, rv, nk, nv, sems
):
    groups = out_ref.shape[0]
    res_rows = rk.shape[1]
    heads = dq.shape[1] // HEAD_SIZE
    tokens = nk.shape[0]
    loads = []
    for g in range(groups):
        rows = pl.ds(16 * g, 16)
        loads.append(
            [
                pltpu.make_async_copy(src.at[rows], dst.at[rows], sems.at[3 * g + i])
                for i, (src, dst) in enumerate(((dq_hbm, dq), (rk_hbm, rk), (rv_hbm, rv)))
            ]
        )
    new_loads = [
        pltpu.make_async_copy(src, dst, sems.at[3 * groups + i])
        for i, (src, dst) in enumerate(((nk_hbm, nk), (nv_hbm, nv)))
    ]
    for copy in loads[0] + new_loads + [copy for group in loads[1:] for copy in group]:
        copy.start()
    base, grp, half_rows = where_ref[0], where_ref[1], where_ref[2]
    keys = 16 * res_rows
    queries = 16 * heads
    col = lax.broadcasted_iota(jnp.int32, (1, keys), 1)
    col_row = col // res_rows
    col_pos = base + col % res_rows
    same_row = (lax.broadcasted_iota(jnp.int32, (queries, keys), 0) % 16) == (
        lax.broadcasted_iota(jnp.int32, (queries, keys), 1) // res_rows
    )
    token = lax.broadcasted_iota(jnp.int32, (1, tokens), 1) - grp * half_rows
    token_bias = jnp.where((token >= 0) & (token < half_rows), 0.0, NEG_FILL)
    for g in range(groups):
        lens = jnp.zeros((1, keys), jnp.int32)
        for r in range(16):
            lens = jnp.where(col_row == r, len_ref[16 * g + r], lens)
        live = jnp.where(col_pos < lens, 0.0, NEG_FILL)
        for copy in loads[g] + (new_loads if g == 0 else []):
            copy.wait()
        q = jnp.concatenate(
            [
                dq[16 * g : 16 * g + 16, h * HEAD_SIZE : (h + 1) * HEAD_SIZE]
                for h in range(heads)
            ],
            axis=0,
        )
        res_k = rk[16 * g : 16 * g + 16].reshape(keys, HEAD_SIZE)
        res_v = rv[16 * g : 16 * g + 16].reshape(keys, HEAD_SIZE)
        s1 = jnp.where(same_row, dot_t(q, res_k) * LOG2_SCALE + live, NEG_FILL)
        s2 = dot_t(q, nk[...]) * LOG2_SCALE + token_bias
        top = jnp.maximum(jnp.max(s1, axis=1, keepdims=True), jnp.max(s2, axis=1, keepdims=True))
        top = top.astype(jnp.bfloat16).astype(jnp.float32)
        p1 = jnp.exp2(s1 - top).astype(jnp.bfloat16)
        p2 = jnp.exp2(s2 - top).astype(jnp.bfloat16)
        total = jnp.sum(p1.astype(jnp.float32), axis=1, keepdims=True) + jnp.sum(
            p2.astype(jnp.float32), axis=1, keepdims=True
        )
        out_ref[g, :queries] = (dot(p1, res_v) + dot(p2, nv[...])).astype(jnp.bfloat16)
        high = total.astype(jnp.bfloat16).astype(jnp.float32)
        stats = as_rows(top) + as_rows(high) + as_rows(total - high)
        stats = jnp.concatenate(stats + [jnp.zeros((10, 128), jnp.float32)], axis=0)
        out_ref[g, queries : queries + 16] = stats.astype(jnp.bfloat16)


def pack_kernel(part_ref, out_ref):
    count = part_ref.shape[0]
    queries = part_ref.shape[1] - 16
    ring, rows = out_ref.shape[0], out_ref.shape[1] // 2
    stats = [part_ref[d, queries : queries + 16].astype(jnp.float32) for d in range(count)]
    top = stats[0][0:2]
    for d in range(1, count):
        top = jnp.maximum(top, stats[d][0:2])
    factors = [jnp.exp2(stats[d][0:2] - top) for d in range(count)]
    total = factors[0] * (stats[0][2:4] + stats[0][4:6])
    for d in range(1, count):
        total = total + factors[d] * (stats[d][2:4] + stats[d][4:6])
    high = total.astype(jnp.bfloat16).astype(jnp.float32)
    columns = factors + [top, high, total - high, jnp.zeros((2, 128), jnp.float32)]
    columns = jnp.concatenate(columns, axis=0).T
    lane = lax.broadcasted_iota(jnp.int32, (128, 128), 1)
    for half in range(2):
        acc = jnp.zeros((128, HEAD_SIZE), jnp.float32)
        for d in range(count):
            part = part_ref[d, 128 * half : 128 * half + 128].astype(jnp.float32)
            acc = acc + part * columns[:, 2 * d + half : 2 * d + half + 1]
        side = jnp.zeros((128, 128), jnp.float32)
        for i in range(3):
            at = 2 * (count + i) + half
            side = jnp.where(lane == i, columns[:, at : at + 1], side)
        out_ref[half * ring // 2 : (half + 1) * ring // 2, :rows] = acc.astype(
            jnp.bfloat16
        ).reshape(ring // 2, rows, HEAD_SIZE)
        out_ref[half * ring // 2 : (half + 1) * ring // 2, rows:] = side.astype(
            jnp.bfloat16
        ).reshape(ring // 2, rows, HEAD_SIZE)


def finish_kernel(part_ref, nk_ref, nv_ref, out_ref):
    tokens = nk_ref.shape[0]
    count = part_ref.shape[0]
    rows = part_ref.shape[1] // 2
    stats = [part_ref[d, rows:].astype(jnp.float32) for d in range(count)]
    top = stats[0][:, 0:1]
    for d in range(1, count):
        top = jnp.maximum(top, stats[d][:, 0:1])
    total = jnp.zeros((rows, 1), jnp.float32)
    acc = jnp.zeros((rows, HEAD_SIZE), jnp.float32)
    for d in range(count):
        factor = jnp.exp2(stats[d][:, 0:1] - top)
        total = total + factor * (stats[d][:, 1:2] + stats[d][:, 2:3])
        acc = acc + factor * part_ref[d, :rows].astype(jnp.float32)
    out_ref[:tokens] = nk_ref[...]
    out_ref[tokens : 2 * tokens] = nv_ref[...]
    out_ref[2 * tokens :] = (acc / total).astype(jnp.bfloat16)


def spread_kernel(tokens, all_ref, out_ref):
    rows = all_ref.shape[1] - 2 * tokens
    for d in range(out_ref.shape[0]):
        for i in range(all_ref.shape[0]):
            out_ref[d, rows * i : rows * (i + 1)] = all_ref[i, 2 * tokens :]


def prefill_kernel(
    where_ref, page_ref, q_ref, own_ref, peer_ref, out_ref, pk_ref, pv_ref, qs, acc, top
):
    ctx, core, bound = where_ref[0], where_ref[1], where_ref[2]
    tokens = q_ref.shape[0]
    heads = q_ref.shape[1] // HEAD_SIZE
    blocks_per = min(4, own_ref.shape[0])
    block = 2 * blocks_per * tokens
    row_block = 2 * tokens
    for s in range(pk_ref.shape[0]):
        source = page_ref[s] // (tokens // PAGE_TOKENS)
        z = source // 2
        row = (page_ref[s] - source * (tokens // PAGE_TOKENS)) * PAGE_TOKENS
        row = pl.multiple_of(row, PAGE_TOKENS)
        value_row = pl.multiple_of(row + tokens, PAGE_TOKENS)
        is_own = source % 2 == core

        @pl.when(is_own)
        def _():
            pk_ref[s] = own_ref[z, pl.ds(row, PAGE_TOKENS), :]
            pv_ref[s] = own_ref[z, pl.ds(value_row, PAGE_TOKENS), :]

        @pl.when(jnp.logical_not(is_own))
        def _():
            pk_ref[s] = peer_ref[z, pl.ds(row, PAGE_TOKENS), :]
            pv_ref[s] = peer_ref[z, pl.ds(value_row, PAGE_TOKENS), :]

    for h in range(heads):
        qs[h * tokens : (h + 1) * tokens] = q_ref[:, h * HEAD_SIZE : (h + 1) * HEAD_SIZE]
    acc[...] = jnp.zeros_like(acc)
    top[...] = jnp.full_like(top, NEG_FILL)
    first = ctx * tokens
    q_pos = first + lax.broadcasted_iota(jnp.int32, (row_block, 1), 0) % tokens
    begin = jnp.where(q_pos < bound, 0, bound)
    col = lax.broadcasted_iota(jnp.int32, (1, block), 1)
    piece = col // tokens
    side = jnp.where(piece < blocks_per, core, 1 - core)
    key_pos0 = (2 * (piece % blocks_per) + side) * tokens + col % tokens
    ones = jnp.ones((block, HEAD_SIZE), jnp.bfloat16)
    lowest = jnp.where(first < bound, 0, bound) // block
    highest = first // block + 1

    def one(step, carry):
        pairs = [(ref, step * blocks_per + i) for ref in (own_ref, peer_ref) for i in range(blocks_per)]
        k = jnp.concatenate([ref[z, :tokens] for ref, z in pairs], axis=0)
        v = jnp.concatenate([ref[z, tokens : 2 * tokens] for ref, z in pairs], axis=0)
        v = jnp.concatenate([v, ones], axis=1)
        key_pos = key_pos0 + step * block
        bias = jnp.where((key_pos <= q_pos) & (key_pos >= begin), 0.0, NEG_FILL)
        for b in range(heads * tokens // row_block):
            rows_b = slice(b * row_block, (b + 1) * row_block)
            s = dot_t(qs[rows_b], k) * LOG2_SCALE + bias
            before = top[rows_b]
            after = jnp.maximum(before, jnp.max(s, axis=1, keepdims=True))
            p = jnp.exp2(s - after).astype(jnp.bfloat16)
            acc[rows_b] = acc[rows_b] * jnp.exp2(before - after) + dot(p, v)
            top[rows_b] = after
        return carry

    lax.fori_loop(lowest, highest, one, 0)
    for h in range(heads):
        rows_h = slice(h * tokens, (h + 1) * tokens)
        out_ref[:, h * HEAD_SIZE : (h + 1) * HEAD_SIZE] = (
            acc[rows_h, :HEAD_SIZE] / acc[rows_h, HEAD_SIZE:]
        ).astype(jnp.bfloat16)


def place_kernel(in_ref, out_ref):
    for g in range(in_ref.shape[0]):
        for h in range(out_ref.shape[1] // HEAD_SIZE):
            out_ref[16 * g : 16 * g + 16, h * HEAD_SIZE : (h + 1) * HEAD_SIZE] = in_ref[
                g, 16 * h : 16 * h + 16
            ]


def local(
    new_queries,
    new_keys,
    new_values,
    segment_ids,
    page_table,
    decode_query_rows,
    resident_keys,
    resident_values,
    res_len,
):
    bf = jnp.bfloat16
    tokens = new_keys.shape[0]
    ring = lax.axis_size("z")
    z, core, grp = (lax.axis_index(a) for a in ("z", "core", "grp"))
    ctx = z * 2 + core
    rows, width = decode_query_rows.shape
    queries = 16 * (width // HEAD_SIZE)
    res_rows = resident_keys.shape[1]
    pages = tokens // PAGE_TOKENS
    i32 = jnp.int32

    where_a = jnp.stack([(ctx * 2 + grp) * res_rows, grp, jnp.int32(tokens // 2)]).astype(i32)
    groups = rows // 16
    part = pl.pallas_call(
        partial_kernel,
        out_shape=jax.ShapeDtypeStruct((groups, queries + 16, HEAD_SIZE), bf),
        in_specs=[SMEM, SMEM] + [HBM] * 5,
        out_specs=VMEM,
        scratch_shapes=[
            pltpu.VMEM(decode_query_rows.shape, bf),
            pltpu.VMEM(resident_keys.shape, bf),
            pltpu.VMEM(resident_values.shape, bf),
            pltpu.VMEM(new_keys.shape, bf),
            pltpu.VMEM(new_values.shape, bf),
            pltpu.SemaphoreType.DMA((3 * groups + 2,)),
        ],
        compiler_params=pltpu.CompilerParams(vmem_limit_bytes=63 * 1024 * 1024),
    )(res_len, where_a, decode_query_rows, resident_keys, resident_values, new_keys, new_values)
    bound = jnp.sum((segment_ids == 0).astype(i32))
    slots = ctx * pages + jnp.arange(pages, dtype=i32)
    ids = jnp.arange(page_table.shape[0], dtype=i32)
    page_from = jnp.sum(jnp.where(page_table[None, :] == slots[:, None], ids[None, :], 0), axis=1)
    where_b = jnp.stack([ctx, core, bound]).astype(i32)
    part = lax.all_to_all(part, ("core", "grp"), 0, 0, tiled=True)
    part, where_b, page_from = lax.optimization_barrier((part, where_b, page_from))
    part = pl.pallas_call(
        pack_kernel,
        out_shape=jax.ShapeDtypeStruct((ring, 2 * queries // ring, HEAD_SIZE), bf),
        in_specs=[VMEM],
        out_specs=VMEM,
        compiler_params=PARAMS,
    )(part)
    part = lax.all_to_all(part, "z", 0, 0, tiled=True)
    packed = pl.pallas_call(
        finish_kernel,
        out_shape=jax.ShapeDtypeStruct((2 * tokens + queries // ring, HEAD_SIZE), bf),
        in_specs=[VMEM] * 3,
        out_specs=VMEM,
        compiler_params=PARAMS,
    )(part, new_keys, new_values)
    kv = lax.all_gather(packed, "z", axis=0)
    peer_kv = lax.ppermute(kv, "core", [(0, 1), (1, 0)])
    dec = pl.pallas_call(
        lambda *refs: spread_kernel(tokens, *refs),
        out_shape=jax.ShapeDtypeStruct((groups, queries, HEAD_SIZE), bf),
        in_specs=[VMEM],
        out_specs=VMEM,
        compiler_params=PARAMS,
    )(kv)
    dec = lax.all_to_all(dec, ("core", "grp"), 0, 0, tiled=True)

    prefill_out, paged_keys, paged_values = pl.pallas_call(
        prefill_kernel,
        out_shape=(
            jax.ShapeDtypeStruct(new_queries.shape, bf),
            jax.ShapeDtypeStruct((pages, PAGE_TOKENS, HEAD_SIZE), bf),
            jax.ShapeDtypeStruct((pages, PAGE_TOKENS, HEAD_SIZE), bf),
        ),
        in_specs=[SMEM, SMEM] + [VMEM] * 3,
        out_specs=(VMEM,) * 3,
        scratch_shapes=[
            pltpu.VMEM((tokens * (new_queries.shape[1] // HEAD_SIZE), HEAD_SIZE), bf),
            pltpu.VMEM(
                (tokens * (new_queries.shape[1] // HEAD_SIZE), 2 * HEAD_SIZE), jnp.float32
            ),
            pltpu.VMEM((tokens * (new_queries.shape[1] // HEAD_SIZE), 1), jnp.float32),
        ],
        compiler_params=PARAMS,
    )(where_b, page_from, new_queries, kv, peer_kv)

    dec = lax.optimization_barrier((dec, paged_keys))[0]
    decode_out = pl.pallas_call(
        place_kernel,
        out_shape=jax.ShapeDtypeStruct((rows, width), bf),
        in_specs=[VMEM],
        out_specs=VMEM,
        compiler_params=PARAMS,
    )(dec)
    return (prefill_out, paged_keys, paged_values, decode_out)


def solution(mesh):
    sizes = mesh.shape
    fine = Mesh(
        np.asarray(mesh.devices).reshape(sizes["ctx"] // 2, 2, sizes["head"], sizes["grp"]),
        ("z", "core", "head", "grp"),
    )
    ctx = ("z", "core")
    return jax.shard_map(
        local,
        mesh=fine,
        in_specs=(
            P(ctx, ("head", "grp")),
            P(ctx, "head"),
            P(ctx, "head"),
            P(),
            P(),
            P(None, "head"),
            P(None, ("z", "core", "grp"), "head"),
            P(None, ("z", "core", "grp"), "head"),
            P(),
        ),
        out_specs=(
            P(ctx, ("head", "grp")),
            P(ctx, None, "head"),
            P(ctx, None, "head"),
            P(None, "head"),
        ),
        check_vma=False,
    )
```

```python
import jax
import jax.numpy as jnp
import numpy as np
from jax import lax
from jax.experimental import pallas as pl
from jax.experimental.pallas import tpu as pltpu
from jax.sharding import Mesh, PartitionSpec as P

HEAD_SIZE = 128
PAGE_TOKENS = 16
NEG_FILL = -1e30
LOG2_SCALE = HEAD_SIZE**-0.5 * 1.4426950408889634
VMEM = pl.BlockSpec(memory_space=pltpu.VMEM)
HBM = pl.BlockSpec(memory_space=pltpu.HBM)
SMEM = pl.BlockSpec(memory_space=pltpu.SMEM)
PARAMS = pltpu.CompilerParams(vmem_limit_bytes=48 * 1024 * 1024)


def dot_t(a, b):
    return lax.dot_general(a, b, (((1,), (1,)), ((), ())), preferred_element_type=jnp.float32)


def dot(a, b):
    return jnp.dot(a, b, preferred_element_type=jnp.float32)


def as_row(column, pick):
    return jnp.sum(jnp.where(pick, column, 0.0), axis=0, keepdims=True)


def partial_kernel(
    len_ref, where_ref, dq_hbm, rk_hbm, rv_hbm, nk_hbm, nv_hbm, out_ref, dq, rk, rv, nk, nv, sems
):
    groups = dq.shape[0] // 16
    res_rows = rk.shape[1]
    heads = dq.shape[1] // HEAD_SIZE
    tokens = nk.shape[0]
    loads = []
    for g in range(groups):
        rows = pl.ds(16 * g, 16)
        loads.append(
            [
                pltpu.make_async_copy(src.at[rows], dst.at[rows], sems.at[3 * g + i])
                for i, (src, dst) in enumerate(((dq_hbm, dq), (rk_hbm, rk), (rv_hbm, rv)))
            ]
        )
    new_loads = [
        pltpu.make_async_copy(src, dst, sems.at[3 * groups + i])
        for i, (src, dst) in enumerate(((nk_hbm, nk), (nv_hbm, nv)))
    ]
    for copy in loads[0] + new_loads + [copy for group in loads[1:] for copy in group]:
        copy.start()
    base, grp, half_rows = where_ref[0], where_ref[1], where_ref[2]
    keys = 16 * res_rows
    queries = 16 * heads
    col = lax.broadcasted_iota(jnp.int32, (1, keys), 1)
    col_row = col // res_rows
    col_pos = base + col % res_rows
    same_row = (lax.broadcasted_iota(jnp.int32, (queries, keys), 0) % 16) == (
        lax.broadcasted_iota(jnp.int32, (queries, keys), 1) // res_rows
    )
    token = lax.broadcasted_iota(jnp.int32, (1, tokens), 1) - grp * half_rows
    token_bias = jnp.where((token >= 0) & (token < half_rows), 0.0, NEG_FILL)
    entry = lax.broadcasted_iota(jnp.int32, (queries, 128), 0)
    lane = lax.broadcasted_iota(jnp.int32, (queries, 128), 1)
    picks = [entry == (lane // 8) * 16 + side * 8 + lane % 8 for side in range(2)]
    for g in range(groups):
        lens = jnp.zeros((1, keys), jnp.int32)
        for r in range(16):
            lens = jnp.where(col_row == r, len_ref[16 * g + r], lens)
        live = jnp.where(col_pos < lens, 0.0, NEG_FILL)
        for copy in loads[g] + (new_loads if g == 0 else []):
            copy.wait()
        q = jnp.concatenate(
            [
                dq[16 * g : 16 * g + 16, h * HEAD_SIZE : (h + 1) * HEAD_SIZE]
                for h in range(heads)
            ],
            axis=0,
        )
        res_k = rk[16 * g : 16 * g + 16].reshape(keys, HEAD_SIZE)
        res_v = rv[16 * g : 16 * g + 16].reshape(keys, HEAD_SIZE)
        s1 = jnp.where(same_row, dot_t(q, res_k) * LOG2_SCALE + live, NEG_FILL)
        s2 = dot_t(q, nk[...]) * LOG2_SCALE + token_bias
        top = jnp.maximum(jnp.max(s1, axis=1, keepdims=True), jnp.max(s2, axis=1, keepdims=True))
        top = top.astype(jnp.bfloat16).astype(jnp.float32)
        p1 = jnp.exp2(s1 - top).astype(jnp.bfloat16)
        p2 = jnp.exp2(s2 - top).astype(jnp.bfloat16)
        total = jnp.sum(p1.astype(jnp.float32), axis=1, keepdims=True) + jnp.sum(
            p2.astype(jnp.float32), axis=1, keepdims=True
        )
        values = (dot(p1, res_v) + dot(p2, nv[...])).reshape(heads, 2, 8, HEAD_SIZE)
        high = total.astype(jnp.bfloat16).astype(jnp.float32)
        for side in range(2):
            stats = [as_row(x, picks[side]) for x in (top, high, total - high)]
            stats = jnp.concatenate(stats + [jnp.zeros((13, 128), jnp.float32)], axis=0)
            at = side * groups + g
            out_ref[at, :128] = values[:, side].reshape(128, HEAD_SIZE).astype(jnp.bfloat16)
            out_ref[at, 128:] = stats.astype(jnp.bfloat16)


def factors_of(stats):
    top = stats[0][0:1]
    for part in stats[1:]:
        top = jnp.maximum(top, part[0:1])
    factors = [jnp.exp2(part[0:1] - top) for part in stats]
    total = factors[0] * (stats[0][1:2] + stats[0][2:3])
    for factor, part in zip(factors[1:], stats[1:]):
        total = total + factor * (part[1:2] + part[2:3])
    return factors, top, total


def pack_kernel(where_ref, part_ref, nk_ref, nv_ref, out_ref):
    tokens = nk_ref.shape[0]
    count = part_ref.shape[0]

    @pl.when(where_ref[1] == 0)
    def _():
        out_ref[:tokens] = nk_ref[...]

    @pl.when(where_ref[1] != 0)
    def _():
        out_ref[:tokens] = nv_ref[...]

    factors, top, total = factors_of(
        [part_ref[d, 128:].astype(jnp.float32) for d in range(count)]
    )
    columns = jnp.concatenate(factors, axis=0).T
    acc = jnp.zeros((128, HEAD_SIZE), jnp.float32)
    for d in range(count):
        acc = acc + part_ref[d, :128].astype(jnp.float32) * columns[:, d : d + 1]
    out_ref[tokens : tokens + 128] = acc.astype(jnp.bfloat16)
    high = total.astype(jnp.bfloat16).astype(jnp.float32)
    stats = [top, high, total - high, jnp.zeros((13, 128), jnp.float32)]
    out_ref[tokens + 128 :] = jnp.concatenate(stats, axis=0).astype(jnp.bfloat16)


def half_kernel(all_ref, out_ref):
    tokens = out_ref.shape[1]
    for d in range(out_ref.shape[0]):
        out_ref[d] = all_ref[d, :tokens]


def finish_kernel(all_ref, out_ref):
    count = all_ref.shape[0]
    begin = all_ref.shape[1] - 144
    sides = []
    for side in range(2):
        parts = range(side, count, 2)
        factors, _, total = factors_of(
            [all_ref[d, begin + 128 :].astype(jnp.float32) for d in parts]
        )
        columns = jnp.concatenate([factor / total for factor in factors], axis=0)
        columns = columns.T
        acc = jnp.zeros((128, HEAD_SIZE), jnp.float32)
        for i, d in enumerate(parts):
            part = all_ref[d, begin : begin + 128].astype(jnp.float32)
            acc = acc + part * columns[:, i : i + 1]
        sides.append(acc.reshape(16, 8, HEAD_SIZE))
    value = jnp.stack(sides, axis=1).reshape(256, HEAD_SIZE).astype(jnp.bfloat16)
    for d in range(out_ref.shape[0]):
        out_ref[d] = value


def prefill_kernel(
    where_ref, page_ref, q_ref, a_own, b_own, a_peer, b_peer, out_ref, pk_ref, pv_ref, qs, acc, top
):
    outs = (out_ref, pk_ref, pv_ref, qs, acc, top)

    @pl.when(where_ref[3] == 0)
    def _():
        attend(where_ref, page_ref, q_ref, a_own, b_own, a_peer, b_peer, *outs)

    @pl.when(where_ref[3] != 0)
    def _():
        attend(where_ref, page_ref, q_ref, b_own, a_own, b_peer, a_peer, *outs)


def attend(where_ref, page_ref, q_ref, k_own, v_own, k_peer, v_peer, out_ref, pk_ref, pv_ref, qs, acc, top):
    ctx, core, bound = where_ref[0], where_ref[1], where_ref[2]
    tokens = q_ref.shape[0]
    heads = q_ref.shape[1] // HEAD_SIZE
    ring = k_own.shape[0]
    blocks_per = min(4, ring)
    block = 2 * blocks_per * tokens
    row_block = 2 * tokens
    for s in range(pk_ref.shape[0]):
        source = page_ref[s] // (tokens // PAGE_TOKENS)
        z = source // 2
        row = (page_ref[s] - source * (tokens // PAGE_TOKENS)) * PAGE_TOKENS
        row = pl.multiple_of(row, PAGE_TOKENS)
        is_own = source % 2 == core

        @pl.when(is_own)
        def _():
            pk_ref[s] = k_own[z, pl.ds(row, PAGE_TOKENS), :]
            pv_ref[s] = v_own[z, pl.ds(row, PAGE_TOKENS), :]

        @pl.when(jnp.logical_not(is_own))
        def _():
            pk_ref[s] = k_peer[z, pl.ds(row, PAGE_TOKENS), :]
            pv_ref[s] = v_peer[z, pl.ds(row, PAGE_TOKENS), :]

    for h in range(heads):
        qs[h * tokens : (h + 1) * tokens] = q_ref[:, h * HEAD_SIZE : (h + 1) * HEAD_SIZE]
    acc[...] = jnp.zeros_like(acc)
    top[...] = jnp.full_like(top, NEG_FILL)
    first = ctx * tokens
    q_pos = first + lax.broadcasted_iota(jnp.int32, (row_block, 1), 0) % tokens
    begin = jnp.where(q_pos < bound, 0, bound)
    col = lax.broadcasted_iota(jnp.int32, (1, block), 1)
    piece = col // tokens
    side = jnp.where(piece < blocks_per, core, 1 - core)
    key_pos0 = (2 * (piece % blocks_per) + side) * tokens + col % tokens
    ones = jnp.ones((block, HEAD_SIZE), jnp.bfloat16)
    lowest = jnp.where(first < bound, 0, bound) // (2 * tokens)
    steps = (ctx // 2 - lowest) // blocks_per + 1

    def one(step, carry):
        low = lowest + step * blocks_per
        places = [jnp.minimum(low + i, ring - 1) for i in range(blocks_per)]
        k = jnp.concatenate([ref[z] for ref in (k_own, k_peer) for z in places], axis=0)
        v = jnp.concatenate([ref[z] for ref in (v_own, v_peer) for z in places], axis=0)
        v = jnp.concatenate([v, ones], axis=1)
        key_pos = key_pos0 + low * (2 * tokens)
        bias = jnp.where((key_pos <= q_pos) & (key_pos >= begin), 0.0, NEG_FILL)
        for b in range(heads * tokens // row_block):
            rows_b = slice(b * row_block, (b + 1) * row_block)
            s = dot_t(qs[rows_b], k) * LOG2_SCALE + bias
            before = top[rows_b]
            after = jnp.maximum(before, jnp.max(s, axis=1, keepdims=True))
            p = jnp.exp2(s - after).astype(jnp.bfloat16)
            acc[rows_b] = acc[rows_b] * jnp.exp2(before - after) + dot(p, v)
            top[rows_b] = after
        return carry

    lax.fori_loop(0, steps, one, 0)
    for h in range(heads):
        rows_h = slice(h * tokens, (h + 1) * tokens)
        out_ref[:, h * HEAD_SIZE : (h + 1) * HEAD_SIZE] = (
            acc[rows_h, :HEAD_SIZE] / acc[rows_h, HEAD_SIZE:]
        ).astype(jnp.bfloat16)


def place_kernel(in_ref, out_ref):
    for g in range(in_ref.shape[0]):
        for h in range(out_ref.shape[1] // HEAD_SIZE):
            out_ref[16 * g : 16 * g + 16, h * HEAD_SIZE : (h + 1) * HEAD_SIZE] = in_ref[
                g, 16 * h : 16 * h + 16
            ]


def local(
    new_queries,
    new_keys,
    new_values,
    segment_ids,
    page_table,
    decode_query_rows,
    resident_keys,
    resident_values,
    res_len,
):
    bf = jnp.bfloat16
    tokens = new_keys.shape[0]
    ring = lax.axis_size("far") * 2
    far, near, core, grp = (lax.axis_index(a) for a in ("far", "near", "core", "grp"))
    ctx = (far * 2 + near) * 2 + core
    rows, width = decode_query_rows.shape
    queries = 16 * (width // HEAD_SIZE)
    res_rows = resident_keys.shape[1]
    pages = tokens // PAGE_TOKENS
    i32 = jnp.int32

    where_a = jnp.stack([(ctx * 2 + grp) * res_rows, grp, jnp.int32(tokens // 2)]).astype(i32)
    groups = rows // 16
    part = pl.pallas_call(
        partial_kernel,
        out_shape=jax.ShapeDtypeStruct((2 * groups, 144, HEAD_SIZE), bf),
        in_specs=[SMEM, SMEM] + [HBM] * 5,
        out_specs=VMEM,
        scratch_shapes=[
            pltpu.VMEM(decode_query_rows.shape, bf),
            pltpu.VMEM(resident_keys.shape, bf),
            pltpu.VMEM(resident_values.shape, bf),
            pltpu.VMEM(new_keys.shape, bf),
            pltpu.VMEM(new_values.shape, bf),
            pltpu.SemaphoreType.DMA((3 * groups + 2,)),
        ],
        compiler_params=pltpu.CompilerParams(vmem_limit_bytes=63 * 1024 * 1024),
    )(res_len, where_a, decode_query_rows, resident_keys, resident_values, new_keys, new_values)
    bound = jnp.sum((segment_ids == 0).astype(i32))
    slots = ctx * pages + jnp.arange(pages, dtype=i32)
    ids = jnp.arange(page_table.shape[0], dtype=i32)
    page_from = jnp.sum(jnp.where(page_table[None, :] == slots[:, None], ids[None, :], 0), axis=1)
    where_b = jnp.stack([ctx, core, bound, grp]).astype(i32)
    part = lax.all_to_all(part, ("near", "core", "grp"), 0, 0, tiled=True)
    part, where_b, page_from = lax.optimization_barrier((part, where_b, page_from))
    packed = pl.pallas_call(
        pack_kernel,
        out_shape=jax.ShapeDtypeStruct((tokens + 144, HEAD_SIZE), bf),
        in_specs=[SMEM] + [VMEM] * 3,
        out_specs=VMEM,
        compiler_params=PARAMS,
    )(where_a, part, new_keys, new_values)
    gathered = lax.all_gather(packed, ("far", "near"), axis=0)
    swap = [(0, 1), (1, 0)]
    a_own = pl.pallas_call(
        half_kernel,
        out_shape=jax.ShapeDtypeStruct((ring, tokens, HEAD_SIZE), bf),
        in_specs=[VMEM],
        out_specs=VMEM,
        compiler_params=PARAMS,
    )(gathered)
    b_own = lax.ppermute(a_own, "grp", swap)
    a_peer = lax.ppermute(a_own, "core", swap)
    dec = pl.pallas_call(
        finish_kernel,
        out_shape=jax.ShapeDtypeStruct((groups, queries, HEAD_SIZE), bf),
        in_specs=[VMEM],
        out_specs=VMEM,
        compiler_params=PARAMS,
    )(gathered)
    b_peer = lax.ppermute(lax.optimization_barrier((b_own, dec))[0], "core", swap)
    dec = lax.all_to_all(dec, ("core", "grp"), 0, 0, tiled=True)

    prefill_out, paged_keys, paged_values = pl.pallas_call(
        prefill_kernel,
        out_shape=(
            jax.ShapeDtypeStruct(new_queries.shape, bf),
            jax.ShapeDtypeStruct((pages, PAGE_TOKENS, HEAD_SIZE), bf),
            jax.ShapeDtypeStruct((pages, PAGE_TOKENS, HEAD_SIZE), bf),
        ),
        in_specs=[SMEM, SMEM] + [VMEM] * 5,
        out_specs=(VMEM,) * 3,
        scratch_shapes=[
            pltpu.VMEM((tokens * (new_queries.shape[1] // HEAD_SIZE), HEAD_SIZE), bf),
            pltpu.VMEM(
                (tokens * (new_queries.shape[1] // HEAD_SIZE), 2 * HEAD_SIZE), jnp.float32
            ),
            pltpu.VMEM((tokens * (new_queries.shape[1] // HEAD_SIZE), 1), jnp.float32),
        ],
        compiler_params=PARAMS,
    )(where_b, page_from, new_queries, a_own, b_own, a_peer, b_peer)

    dec = lax.optimization_barrier((dec, paged_keys))[0]
    decode_out = pl.pallas_call(
        place_kernel,
        out_shape=jax.ShapeDtypeStruct((rows, width), bf),
        in_specs=[VMEM],
        out_specs=VMEM,
        compiler_params=PARAMS,
    )(dec)
    return (prefill_out, paged_keys, paged_values, decode_out)


def solution(mesh):
    sizes = mesh.shape
    fine = Mesh(
        np.asarray(mesh.devices).reshape(
            sizes["ctx"] // 4, 2, 2, sizes["head"], sizes["grp"]
        ),
        ("far", "near", "core", "head", "grp"),
    )
    ctx = ("far", "near", "core")
    return jax.shard_map(
        local,
        mesh=fine,
        in_specs=(
            P(ctx, ("head", "grp")),
            P(ctx, "head"),
            P(ctx, "head"),
            P(),
            P(),
            P(None, "head"),
            P(None, ctx + ("grp",), "head"),
            P(None, ctx + ("grp",), "head"),
            P(),
        ),
        out_specs=(
            P(ctx, ("head", "grp")),
            P(ctx, None, "head"),
            P(ctx, None, "head"),
            P(None, "head"),
        ),
        check_vma=False,
    )
```

```python
import jax
import jax.numpy as jnp
import numpy as np
from jax import lax
from jax.experimental import pallas as pl
from jax.experimental.pallas import tpu as pltpu
from jax.sharding import Mesh, PartitionSpec as P

HEAD_SIZE = 128
PAGE_TOKENS = 16
NEG_FILL = -1e30
LOG2_SCALE = HEAD_SIZE**-0.5 * 1.4426950408889634
VMEM = pl.BlockSpec(memory_space=pltpu.VMEM)
HBM = pl.BlockSpec(memory_space=pltpu.HBM)
SMEM = pl.BlockSpec(memory_space=pltpu.SMEM)
PARAMS = pltpu.CompilerParams(vmem_limit_bytes=48 * 1024 * 1024)


def dot_t(a, b):
    return lax.dot_general(a, b, (((1,), (1,)), ((), ())), preferred_element_type=jnp.float32)


def dot(a, b):
    return jnp.dot(a, b, preferred_element_type=jnp.float32)


def as_row(column, pick):
    return jnp.sum(jnp.where(pick, column, 0.0), axis=0, keepdims=True)


def partial_kernel(
    len_ref, where_ref, dq_hbm, rk_hbm, rv_hbm, nk_hbm, nv_hbm, out_ref, dq, rk, rv, nk, nv, sems
):
    groups = dq.shape[0] // 16
    res_rows = rk.shape[1]
    heads = dq.shape[1] // HEAD_SIZE
    tokens = nk.shape[0]
    loads = []
    for g in range(groups):
        rows = pl.ds(16 * g, 16)
        loads.append(
            [
                pltpu.make_async_copy(src.at[rows], dst.at[rows], sems.at[3 * g + i])
                for i, (src, dst) in enumerate(((dq_hbm, dq), (rk_hbm, rk), (rv_hbm, rv)))
            ]
        )
    new_loads = [
        pltpu.make_async_copy(src, dst, sems.at[3 * groups + i])
        for i, (src, dst) in enumerate(((nk_hbm, nk), (nv_hbm, nv)))
    ]
    for copy in loads[0] + new_loads + [copy for group in loads[1:] for copy in group]:
        copy.start()
    base, grp, half_rows = where_ref[0], where_ref[1], where_ref[2]
    keys = 16 * res_rows
    queries = 16 * heads
    col = lax.broadcasted_iota(jnp.int32, (1, keys), 1)
    col_row = col // res_rows
    col_pos = base + col % res_rows
    same_row = (lax.broadcasted_iota(jnp.int32, (queries, keys), 0) % 16) == (
        lax.broadcasted_iota(jnp.int32, (queries, keys), 1) // res_rows
    )
    token = lax.broadcasted_iota(jnp.int32, (1, tokens), 1) - grp * half_rows
    token_bias = jnp.where((token >= 0) & (token < half_rows), 0.0, NEG_FILL)
    entry = lax.broadcasted_iota(jnp.int32, (queries, 128), 0)
    lane = lax.broadcasted_iota(jnp.int32, (queries, 128), 1)
    picks = [entry == (lane // 8) * 16 + side * 8 + lane % 8 for side in range(2)]
    for g in range(groups):
        lens = jnp.zeros((1, keys), jnp.int32)
        for r in range(16):
            lens = jnp.where(col_row == r, len_ref[16 * g + r], lens)
        live = jnp.where(col_pos < lens, 0.0, NEG_FILL)
        for copy in loads[g] + (new_loads if g == 0 else []):
            copy.wait()
        q = jnp.concatenate(
            [
                dq[16 * g : 16 * g + 16, h * HEAD_SIZE : (h + 1) * HEAD_SIZE]
                for h in range(heads)
            ],
            axis=0,
        )
        res_k = rk[16 * g : 16 * g + 16].reshape(keys, HEAD_SIZE)
        res_v = rv[16 * g : 16 * g + 16].reshape(keys, HEAD_SIZE)
        s1 = jnp.where(same_row, dot_t(q, res_k) * LOG2_SCALE + live, NEG_FILL)
        s2 = dot_t(q, nk[...]) * LOG2_SCALE + token_bias
        top = jnp.maximum(jnp.max(s1, axis=1, keepdims=True), jnp.max(s2, axis=1, keepdims=True))
        top = top.astype(jnp.bfloat16).astype(jnp.float32)
        p1 = jnp.exp2(s1 - top).astype(jnp.bfloat16)
        p2 = jnp.exp2(s2 - top).astype(jnp.bfloat16)
        total = jnp.sum(p1.astype(jnp.float32), axis=1, keepdims=True) + jnp.sum(
            p2.astype(jnp.float32), axis=1, keepdims=True
        )
        values = (dot(p1, res_v) + dot(p2, nv[...])).reshape(heads, 2, 8, HEAD_SIZE)
        high = total.astype(jnp.bfloat16).astype(jnp.float32)
        for side in range(2):
            stats = [as_row(x, picks[side]) for x in (top, high, total - high)]
            stats = jnp.concatenate(stats + [jnp.zeros((13, 128), jnp.float32)], axis=0)
            at = side * groups + g
            out_ref[at, :128] = values[:, side].reshape(128, HEAD_SIZE).astype(jnp.bfloat16)
            out_ref[at, 128:] = stats.astype(jnp.bfloat16)


def factors_of(stats):
    top = stats[0][0:1]
    for part in stats[1:]:
        top = jnp.maximum(top, part[0:1])
    factors = [jnp.exp2(part[0:1] - top) for part in stats]
    total = factors[0] * (stats[0][1:2] + stats[0][2:3])
    for factor, part in zip(factors[1:], stats[1:]):
        total = total + factor * (part[1:2] + part[2:3])
    return factors, top, total


def pack_kernel(where_ref, part_ref, nk_ref, nv_ref, out_ref):
    tokens = nk_ref.shape[0]
    count = part_ref.shape[0]

    half = tokens // 2
    for side in range(2):

        @pl.when(where_ref[1] == side)
        def _():
            out_ref[:half] = nk_ref[side * half : (side + 1) * half]
            out_ref[half:tokens] = nv_ref[side * half : (side + 1) * half]

    factors, top, total = factors_of(
        [part_ref[d, 128:].astype(jnp.float32) for d in range(count)]
    )
    columns = jnp.concatenate(factors, axis=0).T
    acc = jnp.zeros((128, HEAD_SIZE), jnp.float32)
    for d in range(count):
        acc = acc + part_ref[d, :128].astype(jnp.float32) * columns[:, d : d + 1]
    out_ref[tokens : tokens + 128] = acc.astype(jnp.bfloat16)
    high = total.astype(jnp.bfloat16).astype(jnp.float32)
    stats = [top, high, total - high, jnp.zeros((13, 128), jnp.float32)]
    out_ref[tokens + 128 :] = jnp.concatenate(stats, axis=0).astype(jnp.bfloat16)


def finish_kernel(all_ref, out_ref):
    count = all_ref.shape[0]
    begin = all_ref.shape[1] - 144
    for d in range(count):
        out_ref[begin * d : begin * (d + 1)] = all_ref[d, :begin]
    sides = []
    for side in range(2):
        parts = range(side, count, 2)
        factors, _, total = factors_of(
            [all_ref[d, begin + 128 :].astype(jnp.float32) for d in parts]
        )
        columns = jnp.concatenate([factor / total for factor in factors], axis=0)
        columns = columns.T
        acc = jnp.zeros((128, HEAD_SIZE), jnp.float32)
        for i, d in enumerate(parts):
            part = all_ref[d, begin : begin + 128].astype(jnp.float32)
            acc = acc + part * columns[:, i : i + 1]
        sides.append(acc.reshape(16, 8, HEAD_SIZE))
    value = jnp.stack(sides, axis=1).reshape(256, HEAD_SIZE).astype(jnp.bfloat16)
    out_ref[begin * count :] = value


def attend(where_ref, grp, own_ref, peer_ref, qs, acc, top):
    ctx, core, bound = where_ref[0], where_ref[1], where_ref[2]
    tokens = 96
    half = tokens // 2
    ring = own_ref.shape[0] // tokens
    blocks_per = min(8, ring)
    block = 2 * blocks_per * half
    row_block = 2 * tokens
    first = ctx * tokens
    q_pos = first + lax.broadcasted_iota(jnp.int32, (row_block, 1), 0) % tokens
    begin = jnp.where(q_pos < bound, 0, bound)
    col = lax.broadcasted_iota(jnp.int32, (1, block), 1)
    piece = col // half
    side = jnp.where(piece < blocks_per, core, 1 - core)
    key_pos0 = (2 * (piece % blocks_per) + side) * tokens + grp * half + col % half
    ones = jnp.ones((block, HEAD_SIZE), jnp.bfloat16)
    lowest = jnp.where(first < bound, 0, bound) // (2 * tokens)
    steps = (ctx // 2 - lowest) // blocks_per + 1

    def one(step, carry):
        low = lowest + step * blocks_per
        places = [
            pl.multiple_of(jnp.minimum(low + i, ring - 1) * tokens, PAGE_TOKENS)
            for i in range(blocks_per)
        ]
        k = jnp.concatenate(
            [ref[pl.ds(z, half), :] for ref in (own_ref, peer_ref) for z in places], axis=0
        )
        v = jnp.concatenate(
            [
                ref[pl.ds(pl.multiple_of(z + half, PAGE_TOKENS), half), :]
                for ref in (own_ref, peer_ref)
                for z in places
            ],
            axis=0,
        )
        v = jnp.concatenate([v, ones], axis=1)
        key_pos = key_pos0 + low * (2 * tokens)
        bias = jnp.where((key_pos <= q_pos) & (key_pos >= begin), 0.0, NEG_FILL)
        for b in range(qs.shape[0] // row_block):
            rows_b = slice(b * row_block, (b + 1) * row_block)
            s = dot_t(qs[rows_b], k) * LOG2_SCALE + bias
            before = top[rows_b]
            after = jnp.maximum(before, jnp.max(s, axis=1, keepdims=True))
            p = jnp.exp2(s - after).astype(jnp.bfloat16)
            acc[rows_b] = acc[rows_b] * jnp.exp2(before - after) + dot(p, v)
            top[rows_b] = after
        return carry

    lax.fori_loop(0, steps, one, 0)


def first_kernel(where_ref, q_ref, own_ref, peer_ref, qs, acc, top):
    tokens = q_ref.shape[0]
    for h in range(q_ref.shape[1] // HEAD_SIZE):
        qs[h * tokens : (h + 1) * tokens] = q_ref[:, h * HEAD_SIZE : (h + 1) * HEAD_SIZE]
    acc[...] = jnp.zeros_like(acc)
    top[...] = jnp.full_like(top, NEG_FILL)
    attend(where_ref, where_ref[3], own_ref, peer_ref, qs, acc, top)


def second_kernel(
    where_ref, page_ref, a_own, a_peer, b_own, b_peer, qs, acc_in, top_in,
    out_ref, pk_ref, pv_ref, dec_ref, acc, top,
):
    ctx, core, grp = where_ref[0], where_ref[1], where_ref[3]
    tokens = out_ref.shape[0]
    heads = out_ref.shape[1] // HEAD_SIZE
    half = tokens // 2
    pages = tokens // PAGE_TOKENS
    for s in range(pk_ref.shape[0]):
        source = page_ref[s] // pages
        page = page_ref[s] - source * pages
        side = page // (pages // 2)
        row = (source // 2) * tokens + (page - side * (pages // 2)) * PAGE_TOKENS
        row = pl.multiple_of(row, PAGE_TOKENS)
        value_row = pl.multiple_of(row + half, PAGE_TOKENS)
        for same_side, same_core, ref in (
            (True, True, a_own), (True, False, a_peer), (False, True, b_own), (False, False, b_peer),
        ):
            there = ((side == grp) == same_side) & ((source % 2 == core) == same_core)

            @pl.when(there)
            def _():
                pk_ref[s] = ref[pl.ds(row, PAGE_TOKENS), :]
                pv_ref[s] = ref[pl.ds(value_row, PAGE_TOKENS), :]

    columns = dec_ref.shape[1] // HEAD_SIZE
    begin = a_own.shape[0] - 16 * columns
    for at_core, at_grp, ref in (
        (core, grp, a_own), (1 - core, grp, a_peer), (core, 1 - grp, b_own), (1 - core, 1 - grp, b_peer),
    ):
        row = pl.multiple_of((at_core * 2 + at_grp) * 16, 16)
        for h in range(columns):
            dec_ref[pl.ds(row, 16), h * HEAD_SIZE : (h + 1) * HEAD_SIZE] = ref[
                begin + 16 * h : begin + 16 * h + 16
            ]
    acc[...] = acc_in[...]
    top[...] = top_in[...]
    attend(where_ref, 1 - grp, b_own, b_peer, qs, acc, top)
    for h in range(heads):
        rows_h = slice(h * tokens, (h + 1) * tokens)
        out_ref[:, h * HEAD_SIZE : (h + 1) * HEAD_SIZE] = (
            acc[rows_h, :HEAD_SIZE] / acc[rows_h, HEAD_SIZE:]
        ).astype(jnp.bfloat16)


def local(
    new_queries,
    new_keys,
    new_values,
    segment_ids,
    page_table,
    decode_query_rows,
    resident_keys,
    resident_values,
    res_len,
):
    bf = jnp.bfloat16
    tokens = new_keys.shape[0]
    ring = lax.axis_size("far") * 2
    far, near, core, grp = (lax.axis_index(a) for a in ("far", "near", "core", "grp"))
    ctx = (far * 2 + near) * 2 + core
    rows, width = decode_query_rows.shape
    queries = 16 * (width // HEAD_SIZE)
    res_rows = resident_keys.shape[1]
    pages = tokens // PAGE_TOKENS
    i32 = jnp.int32

    where_a = jnp.stack([(ctx * 2 + grp) * res_rows, grp, jnp.int32(tokens // 2)]).astype(i32)
    groups = rows // 16
    part = pl.pallas_call(
        partial_kernel,
        out_shape=jax.ShapeDtypeStruct((2 * groups, 144, HEAD_SIZE), bf),
        in_specs=[SMEM, SMEM] + [HBM] * 5,
        out_specs=VMEM,
        scratch_shapes=[
            pltpu.VMEM(decode_query_rows.shape, bf),
            pltpu.VMEM(resident_keys.shape, bf),
            pltpu.VMEM(resident_values.shape, bf),
            pltpu.VMEM(new_keys.shape, bf),
            pltpu.VMEM(new_values.shape, bf),
            pltpu.SemaphoreType.DMA((3 * groups + 2,)),
        ],
        compiler_params=pltpu.CompilerParams(vmem_limit_bytes=63 * 1024 * 1024),
    )(res_len, where_a, decode_query_rows, resident_keys, resident_values, new_keys, new_values)
    bound = jnp.sum((segment_ids == 0).astype(i32))
    slots = ctx * pages + jnp.arange(pages, dtype=i32)
    ids = jnp.arange(page_table.shape[0], dtype=i32)
    page_from = jnp.sum(jnp.where(page_table[None, :] == slots[:, None], ids[None, :], 0), axis=1)
    where_b = jnp.stack([ctx, core, bound, grp]).astype(i32)
    part = lax.all_to_all(part, ("near", "core", "grp"), 0, 0, tiled=True)
    part, where_b, page_from = lax.optimization_barrier((part, where_b, page_from))
    packed = pl.pallas_call(
        pack_kernel,
        out_shape=jax.ShapeDtypeStruct((tokens + 144, HEAD_SIZE), bf),
        in_specs=[SMEM] + [VMEM] * 3,
        out_specs=VMEM,
        compiler_params=PARAMS,
    )(where_a, part, new_keys, new_values)
    gathered = lax.all_gather(packed, ("far", "near"), axis=0)
    swap = [(0, 1), (1, 0)]
    a_own = pl.pallas_call(
        finish_kernel,
        out_shape=jax.ShapeDtypeStruct((ring * tokens + queries, HEAD_SIZE), bf),
        in_specs=[VMEM],
        out_specs=VMEM,
        compiler_params=PARAMS,
    )(gathered)
    b_own = lax.ppermute(a_own, "grp", swap)
    a_peer = lax.ppermute(a_own, "core", swap)
    b_peer = lax.ppermute(b_own, "core", swap)
    stacked = tokens * (new_queries.shape[1] // HEAD_SIZE)
    state = pl.pallas_call(
        first_kernel,
        out_shape=(
            jax.ShapeDtypeStruct((stacked, HEAD_SIZE), bf),
            jax.ShapeDtypeStruct((stacked, 2 * HEAD_SIZE), jnp.float32),
            jax.ShapeDtypeStruct((stacked, 1), jnp.float32),
        ),
        in_specs=[SMEM] + [VMEM] * 3,
        out_specs=(VMEM,) * 3,
        compiler_params=PARAMS,
    )(where_b, new_queries, a_own, a_peer)
    prefill_out, paged_keys, paged_values, decode_out = pl.pallas_call(
        second_kernel,
        out_shape=(
            jax.ShapeDtypeStruct(new_queries.shape, bf),
            jax.ShapeDtypeStruct((pages, PAGE_TOKENS, HEAD_SIZE), bf),
            jax.ShapeDtypeStruct((pages, PAGE_TOKENS, HEAD_SIZE), bf),
            jax.ShapeDtypeStruct((rows, width), bf),
        ),
        in_specs=[SMEM, SMEM] + [VMEM] * 7,
        out_specs=(VMEM,) * 4,
        scratch_shapes=[
            pltpu.VMEM((stacked, 2 * HEAD_SIZE), jnp.float32),
            pltpu.VMEM((stacked, 1), jnp.float32),
        ],
        compiler_params=PARAMS,
    )(where_b, page_from, a_own, a_peer, b_own, b_peer, *state)
    return (prefill_out, paged_keys, paged_values, decode_out)


def solution(mesh):
    sizes = mesh.shape
    fine = Mesh(
        np.asarray(mesh.devices).reshape(
            sizes["ctx"] // 4, 2, 2, sizes["head"], sizes["grp"]
        ),
        ("far", "near", "core", "head", "grp"),
    )
    ctx = ("far", "near", "core")
    return jax.shard_map(
        local,
        mesh=fine,
        in_specs=(
            P(ctx, ("head", "grp")),
            P(ctx, "head"),
            P(ctx, "head"),
            P(),
            P(),
            P(None, "head"),
            P(None, ctx + ("grp",), "head"),
            P(None, ctx + ("grp",), "head"),
            P(),
        ),
        out_specs=(
            P(ctx, ("head", "grp")),
            P(ctx, None, "head"),
            P(ctx, None, "head"),
            P(None, "head"),
        ),
        check_vma=False,
    )
```

```python
import jax
import jax.numpy as jnp
import numpy as np
from jax import lax
from jax.experimental import pallas as pl
from jax.experimental.pallas import tpu as pltpu
from jax.sharding import Mesh, PartitionSpec as P

HEAD_SIZE = 128
PAGE_TOKENS = 16
NEG_FILL = -1e30
LOG2_SCALE = HEAD_SIZE**-0.5 * 1.4426950408889634
VMEM = pl.BlockSpec(memory_space=pltpu.VMEM)
HBM = pl.BlockSpec(memory_space=pltpu.HBM)
SMEM = pl.BlockSpec(memory_space=pltpu.SMEM)
PARAMS = pltpu.CompilerParams(vmem_limit_bytes=48 * 1024 * 1024)


def dot_t(a, b):
    return lax.dot_general(a, b, (((1,), (1,)), ((), ())), preferred_element_type=jnp.float32)


def dot(a, b):
    return jnp.dot(a, b, preferred_element_type=jnp.float32)


def as_row(column, pick):
    return jnp.sum(jnp.where(pick, column, 0.0), axis=0, keepdims=True)


def partial_kernel(
    len_ref, dq_hbm, rk_hbm, rv_hbm, nk_hbm, nv_hbm, out_ref, dq, rk, rv, nk, nv, sems
):
    groups = dq.shape[0] // 16
    res_rows = rk.shape[1]
    heads = dq.shape[1] // HEAD_SIZE
    tokens = nk.shape[0]
    loads = []
    for g in range(groups):
        rows = pl.ds(16 * g, 16)
        loads.append(
            [
                pltpu.make_async_copy(src.at[rows], dst.at[rows], sems.at[3 * g + i])
                for i, (src, dst) in enumerate(((dq_hbm, dq), (rk_hbm, rk), (rv_hbm, rv)))
            ]
        )
    new_loads = [
        pltpu.make_async_copy(src, dst, sems.at[3 * groups + i])
        for i, (src, dst) in enumerate(((nk_hbm, nk), (nv_hbm, nv)))
    ]
    for copy in loads[0] + new_loads + [copy for group in loads[1:] for copy in group]:
        copy.start()
    grp = lax.axis_index("grp")
    place = (lax.axis_index("far") * 2 + lax.axis_index("near")) * 2 + lax.axis_index("core")
    base = (place * 2 + grp) * res_rows
    half_rows = tokens // 2
    keys = 16 * res_rows
    queries = 16 * heads
    col = lax.broadcasted_iota(jnp.int32, (1, keys), 1)
    col_row = col // res_rows
    col_pos = base + col % res_rows
    same_row = (lax.broadcasted_iota(jnp.int32, (queries, keys), 0) % 16) == (
        lax.broadcasted_iota(jnp.int32, (queries, keys), 1) // res_rows
    )
    token = lax.broadcasted_iota(jnp.int32, (1, tokens), 1) - grp * half_rows
    token_bias = jnp.where((token >= 0) & (token < half_rows), 0.0, NEG_FILL)
    entry = lax.broadcasted_iota(jnp.int32, (queries, 128), 0)
    lane = lax.broadcasted_iota(jnp.int32, (queries, 128), 1)
    picks = [entry == (lane // 8) * 16 + side * 8 + lane % 8 for side in range(2)]
    for g in range(groups):
        lens = jnp.zeros((1, keys), jnp.int32)
        for r in range(16):
            lens = jnp.where(col_row == r, len_ref[16 * g + r], lens)
        live = jnp.where(col_pos < lens, 0.0, NEG_FILL)
        for copy in loads[g] + (new_loads if g == 0 else []):
            copy.wait()
        q = jnp.concatenate(
            [
                dq[16 * g : 16 * g + 16, h * HEAD_SIZE : (h + 1) * HEAD_SIZE]
                for h in range(heads)
            ],
            axis=0,
        )
        res_k = rk[16 * g : 16 * g + 16].reshape(keys, HEAD_SIZE)
        res_v = rv[16 * g : 16 * g + 16].reshape(keys, HEAD_SIZE)
        s1 = jnp.where(same_row, dot_t(q, res_k) * LOG2_SCALE + live, NEG_FILL)
        s2 = dot_t(q, nk[...]) * LOG2_SCALE + token_bias
        top = jnp.maximum(jnp.max(s1, axis=1, keepdims=True), jnp.max(s2, axis=1, keepdims=True))
        top = top.astype(jnp.bfloat16).astype(jnp.float32)
        p1 = jnp.exp2(s1 - top).astype(jnp.bfloat16)
        p2 = jnp.exp2(s2 - top).astype(jnp.bfloat16)
        total = jnp.sum(p1.astype(jnp.float32), axis=1, keepdims=True) + jnp.sum(
            p2.astype(jnp.float32), axis=1, keepdims=True
        )
        values = (dot(p1, res_v) + dot(p2, nv[...])).reshape(heads, 2, 8, HEAD_SIZE)
        high = total.astype(jnp.bfloat16).astype(jnp.float32)
        for side in range(2):
            stats = [as_row(x, picks[side]) for x in (top, high, total - high)]
            stats = jnp.concatenate(stats + [jnp.zeros((13, 128), jnp.float32)], axis=0)
            at = side * groups + g
            out_ref[at, :128] = values[:, side].reshape(128, HEAD_SIZE).astype(jnp.bfloat16)
            out_ref[at, 128:] = stats.astype(jnp.bfloat16)


def factors_of(stats):
    top = stats[0][0:1]
    for part in stats[1:]:
        top = jnp.maximum(top, part[0:1])
    factors = [jnp.exp2(part[0:1] - top) for part in stats]
    total = factors[0] * (stats[0][1:2] + stats[0][2:3])
    for factor, part in zip(factors[1:], stats[1:]):
        total = total + factor * (part[1:2] + part[2:3])
    return factors, top, total


def pack_kernel(part_ref, nk_ref, nv_ref, out_ref):
    tokens = nk_ref.shape[0]
    count = part_ref.shape[0]

    half = tokens // 2
    for side in range(2):

        @pl.when(lax.axis_index("grp") == side)
        def _():
            out_ref[:half] = nk_ref[side * half : (side + 1) * half]
            out_ref[half:tokens] = nv_ref[side * half : (side + 1) * half]

    factors, top, total = factors_of(
        [part_ref[d, 128:].astype(jnp.float32) for d in range(count)]
    )
    columns = jnp.concatenate(factors, axis=0).T
    acc = jnp.zeros((128, HEAD_SIZE), jnp.float32)
    for d in range(count):
        acc = acc + part_ref[d, :128].astype(jnp.float32) * columns[:, d : d + 1]
    out_ref[tokens : tokens + 128] = acc.astype(jnp.bfloat16)
    high = total.astype(jnp.bfloat16).astype(jnp.float32)
    stats = [top, high, total - high, jnp.zeros((13, 128), jnp.float32)]
    out_ref[tokens + 128 :] = jnp.concatenate(stats, axis=0).astype(jnp.bfloat16)


def finish_kernel(all_ref, out_ref):
    count = all_ref.shape[0]
    begin = all_ref.shape[1] - 144
    for d in range(count):
        out_ref[begin * d : begin * (d + 1)] = all_ref[d, :begin]
    sides = []
    for side in range(2):
        parts = range(side, count, 2)
        factors, _, total = factors_of(
            [all_ref[d, begin + 128 :].astype(jnp.float32) for d in parts]
        )
        columns = jnp.concatenate([factor / total for factor in factors], axis=0)
        columns = columns.T
        acc = jnp.zeros((128, HEAD_SIZE), jnp.float32)
        for i, d in enumerate(parts):
            part = all_ref[d, begin : begin + 128].astype(jnp.float32)
            acc = acc + part * columns[:, i : i + 1]
        sides.append(acc.reshape(16, 8, HEAD_SIZE))
    value = jnp.stack(sides, axis=1).reshape(256, HEAD_SIZE).astype(jnp.bfloat16)
    out_ref[begin * count :] = value


def attend(where_ref, grp, own_ref, peer_ref, qs, acc, top):
    ctx, core, bound = where_ref[0], where_ref[1], where_ref[2]
    tokens = 96
    half = tokens // 2
    ring = own_ref.shape[0] // tokens
    blocks_per = min(8, ring)
    block = 2 * blocks_per * half
    row_block = 2 * tokens
    first = ctx * tokens
    q_pos = first + lax.broadcasted_iota(jnp.int32, (row_block, 1), 0) % tokens
    begin = jnp.where(q_pos < bound, 0, bound)
    col = lax.broadcasted_iota(jnp.int32, (1, block), 1)
    piece = col // half
    side = jnp.where(piece < blocks_per, core, 1 - core)
    key_pos0 = (2 * (piece % blocks_per) + side) * tokens + grp * half + col % half
    ones = jnp.ones((block, HEAD_SIZE), jnp.bfloat16)
    lowest = jnp.where(first < bound, 0, bound) // (2 * tokens)
    steps = (ctx // 2 - lowest) // blocks_per + 1

    def one(step, carry):
        low = lowest + step * blocks_per
        places = [
            pl.multiple_of(jnp.minimum(low + i, ring - 1) * tokens, PAGE_TOKENS)
            for i in range(blocks_per)
        ]
        k = jnp.concatenate(
            [ref[pl.ds(z, half), :] for ref in (own_ref, peer_ref) for z in places], axis=0
        )
        v = jnp.concatenate(
            [
                ref[pl.ds(pl.multiple_of(z + half, PAGE_TOKENS), half), :]
                for ref in (own_ref, peer_ref)
                for z in places
            ],
            axis=0,
        )
        v = jnp.concatenate([v, ones], axis=1)
        key_pos = key_pos0 + low * (2 * tokens)
        bias = jnp.where((key_pos <= q_pos) & (key_pos >= begin), 0.0, NEG_FILL)
        for b in range(qs.shape[0] // row_block):
            rows_b = slice(b * row_block, (b + 1) * row_block)
            s = dot_t(qs[rows_b], k) * LOG2_SCALE + bias
            before = top[rows_b]
            after = jnp.maximum(before, jnp.max(s, axis=1, keepdims=True))
            p = jnp.exp2(s - after).astype(jnp.bfloat16)
            acc[rows_b] = acc[rows_b] * jnp.exp2(before - after) + dot(p, v)
            top[rows_b] = after
        return carry

    lax.fori_loop(0, steps, one, 0)


def first_kernel(where_ref, q_ref, own_ref, peer_ref, qs, acc, top):
    tokens = q_ref.shape[0]
    for h in range(q_ref.shape[1] // HEAD_SIZE):
        qs[h * tokens : (h + 1) * tokens] = q_ref[:, h * HEAD_SIZE : (h + 1) * HEAD_SIZE]
    acc[...] = jnp.zeros_like(acc)
    top[...] = jnp.full_like(top, NEG_FILL)
    attend(where_ref, where_ref[3], own_ref, peer_ref, qs, acc, top)


def second_kernel(
    where_ref, page_ref, a_own, a_peer, b_own, b_peer, qs, acc_in, top_in,
    out_ref, pk_ref, pv_ref, dec_ref, acc, top,
):
    ctx, core, grp = where_ref[0], where_ref[1], where_ref[3]
    tokens = out_ref.shape[0]
    heads = out_ref.shape[1] // HEAD_SIZE
    half = tokens // 2
    pages = tokens // PAGE_TOKENS
    for s in range(pk_ref.shape[0]):
        source = page_ref[s] // pages
        page = page_ref[s] - source * pages
        side = page // (pages // 2)
        row = (source // 2) * tokens + (page - side * (pages // 2)) * PAGE_TOKENS
        row = pl.multiple_of(row, PAGE_TOKENS)
        value_row = pl.multiple_of(row + half, PAGE_TOKENS)
        for same_side, same_core, ref in (
            (True, True, a_own), (True, False, a_peer), (False, True, b_own), (False, False, b_peer),
        ):
            there = ((side == grp) == same_side) & ((source % 2 == core) == same_core)

            @pl.when(there)
            def _():
                pk_ref[s] = ref[pl.ds(row, PAGE_TOKENS), :]
                pv_ref[s] = ref[pl.ds(value_row, PAGE_TOKENS), :]

    columns = dec_ref.shape[1] // HEAD_SIZE
    begin = a_own.shape[0] - 16 * columns
    for at_core, at_grp, ref in (
        (core, grp, a_own), (1 - core, grp, a_peer), (core, 1 - grp, b_own), (1 - core, 1 - grp, b_peer),
    ):
        row = pl.multiple_of((at_core * 2 + at_grp) * 16, 16)
        for h in range(columns):
            dec_ref[pl.ds(row, 16), h * HEAD_SIZE : (h + 1) * HEAD_SIZE] = ref[
                begin + 16 * h : begin + 16 * h + 16
            ]
    acc[...] = acc_in[...]
    top[...] = top_in[...]
    attend(where_ref, 1 - grp, b_own, b_peer, qs, acc, top)
    for h in range(heads):
        rows_h = slice(h * tokens, (h + 1) * tokens)
        out_ref[:, h * HEAD_SIZE : (h + 1) * HEAD_SIZE] = (
            acc[rows_h, :HEAD_SIZE] / acc[rows_h, HEAD_SIZE:]
        ).astype(jnp.bfloat16)


def local(
    new_queries,
    new_keys,
    new_values,
    segment_ids,
    page_table,
    decode_query_rows,
    resident_keys,
    resident_values,
    res_len,
):
    bf = jnp.bfloat16
    tokens = new_keys.shape[0]
    ring = lax.axis_size("far") * 2
    far, near, core, grp = (lax.axis_index(a) for a in ("far", "near", "core", "grp"))
    ctx = (far * 2 + near) * 2 + core
    rows, width = decode_query_rows.shape
    queries = 16 * (width // HEAD_SIZE)
    res_rows = resident_keys.shape[1]
    pages = tokens // PAGE_TOKENS
    i32 = jnp.int32

    groups = rows // 16
    part = pl.pallas_call(
        partial_kernel,
        out_shape=jax.ShapeDtypeStruct((2 * groups, 144, HEAD_SIZE), bf),
        in_specs=[SMEM] + [HBM] * 5,
        out_specs=VMEM,
        scratch_shapes=[
            pltpu.VMEM(decode_query_rows.shape, bf),
            pltpu.VMEM(resident_keys.shape, bf),
            pltpu.VMEM(resident_values.shape, bf),
            pltpu.VMEM(new_keys.shape, bf),
            pltpu.VMEM(new_values.shape, bf),
            pltpu.SemaphoreType.DMA((3 * groups + 2,)),
        ],
        compiler_params=pltpu.CompilerParams(vmem_limit_bytes=63 * 1024 * 1024),
    )(res_len, decode_query_rows, resident_keys, resident_values, new_keys, new_values)
    bound = jnp.sum((segment_ids == 0).astype(i32))
    slots = ctx * pages + jnp.arange(pages, dtype=i32)
    ids = jnp.arange(page_table.shape[0], dtype=i32)
    page_from = jnp.sum(jnp.where(page_table[None, :] == slots[:, None], ids[None, :], 0), axis=1)
    where_b = jnp.stack([ctx, core, bound, grp]).astype(i32)
    part = lax.all_to_all(part, ("near", "core", "grp"), 0, 0, tiled=True)
    part, where_b, page_from = lax.optimization_barrier((part, where_b, page_from))
    packed = pl.pallas_call(
        pack_kernel,
        out_shape=jax.ShapeDtypeStruct((tokens + 144, HEAD_SIZE), bf),
        in_specs=[VMEM] * 3,
        out_specs=VMEM,
        compiler_params=PARAMS,
    )(part, new_keys, new_values)
    gathered = lax.all_gather(packed, ("far", "near"), axis=0)
    swap = [(0, 1), (1, 0)]
    a_own = pl.pallas_call(
        finish_kernel,
        out_shape=jax.ShapeDtypeStruct((ring * tokens + queries, HEAD_SIZE), bf),
        in_specs=[VMEM],
        out_specs=VMEM,
        compiler_params=PARAMS,
    )(gathered)
    b_own = lax.ppermute(a_own, "grp", swap)
    a_peer = lax.ppermute(a_own, "core", swap)
    b_peer = lax.ppermute(b_own, "core", swap)
    stacked = tokens * (new_queries.shape[1] // HEAD_SIZE)
    state = pl.pallas_call(
        first_kernel,
        out_shape=(
            jax.ShapeDtypeStruct((stacked, HEAD_SIZE), bf),
            jax.ShapeDtypeStruct((stacked, 2 * HEAD_SIZE), jnp.float32),
            jax.ShapeDtypeStruct((stacked, 1), jnp.float32),
        ),
        in_specs=[SMEM] + [VMEM] * 3,
        out_specs=(VMEM,) * 3,
        compiler_params=PARAMS,
    )(where_b, new_queries, a_own, a_peer)
    prefill_out, paged_keys, paged_values, decode_out = pl.pallas_call(
        second_kernel,
        out_shape=(
            jax.ShapeDtypeStruct(new_queries.shape, bf),
            jax.ShapeDtypeStruct((pages, PAGE_TOKENS, HEAD_SIZE), bf),
            jax.ShapeDtypeStruct((pages, PAGE_TOKENS, HEAD_SIZE), bf),
            jax.ShapeDtypeStruct((rows, width), bf),
        ),
        in_specs=[SMEM, SMEM] + [VMEM] * 7,
        out_specs=(VMEM,) * 4,
        scratch_shapes=[
            pltpu.VMEM((stacked, 2 * HEAD_SIZE), jnp.float32),
            pltpu.VMEM((stacked, 1), jnp.float32),
        ],
        compiler_params=PARAMS,
    )(where_b, page_from, a_own, a_peer, b_own, b_peer, *state)
    return (prefill_out, paged_keys, paged_values, decode_out)


def solution(mesh):
    sizes = mesh.shape
    fine = Mesh(
        np.asarray(mesh.devices).reshape(
            sizes["ctx"] // 4, 2, 2, sizes["head"], sizes["grp"]
        ),
        ("far", "near", "core", "head", "grp"),
    )
    ctx = ("far", "near", "core")
    return jax.shard_map(
        local,
        mesh=fine,
        in_specs=(
            P(ctx, ("head", "grp")),
            P(ctx, "head"),
            P(ctx, "head"),
            P(),
            P(),
            P(None, "head"),
            P(None, ctx + ("grp",), "head"),
            P(None, ctx + ("grp",), "head"),
            P(),
        ),
        out_specs=(
            P(ctx, ("head", "grp")),
            P(ctx, None, "head"),
            P(ctx, None, "head"),
            P(None, "head"),
        ),
        check_vma=False,
    )
```

```python
import jax
import jax.numpy as jnp
import numpy as np
from jax import lax
from jax.experimental import pallas as pl
from jax.experimental.pallas import tpu as pltpu
from jax.sharding import Mesh, PartitionSpec as P

HEAD_SIZE = 128
PAGE_TOKENS = 16
NEG_FILL = -1e30
LOG2_SCALE = HEAD_SIZE**-0.5 * 1.4426950408889634
VMEM = pl.BlockSpec(memory_space=pltpu.VMEM)
HBM = pl.BlockSpec(memory_space=pltpu.HBM)
SMEM = pl.BlockSpec(memory_space=pltpu.SMEM)
PARAMS = pltpu.CompilerParams(vmem_limit_bytes=48 * 1024 * 1024)


def dot_t(a, b):
    return lax.dot_general(a, b, (((1,), (1,)), ((), ())), preferred_element_type=jnp.float32)


def dot(a, b):
    return jnp.dot(a, b, preferred_element_type=jnp.float32)


def as_row(column, pick):
    return jnp.sum(jnp.where(pick, column, 0.0), axis=0, keepdims=True)


def partial_kernel(
    len_ref, dq_hbm, rk_hbm, rv_hbm, nk_hbm, nv_hbm, out_ref, dq, rk, rv, nk, nv, sems
):
    groups = dq.shape[0] // 16
    res_rows = rk.shape[1]
    heads = dq.shape[1] // HEAD_SIZE
    tokens = nk.shape[0]
    loads = []
    for g in range(groups):
        rows = pl.ds(16 * g, 16)
        loads.append(
            [
                pltpu.make_async_copy(src.at[rows], dst.at[rows], sems.at[3 * g + i])
                for i, (src, dst) in enumerate(((dq_hbm, dq), (rk_hbm, rk), (rv_hbm, rv)))
            ]
        )
    new_loads = [
        pltpu.make_async_copy(src, dst, sems.at[3 * groups + i])
        for i, (src, dst) in enumerate(((nk_hbm, nk), (nv_hbm, nv)))
    ]
    for copy in loads[0] + new_loads + [copy for group in loads[1:] for copy in group]:
        copy.start()
    grp = lax.axis_index("grp")
    place = (lax.axis_index("far") * 2 + lax.axis_index("near")) * 2 + lax.axis_index("core")
    base = (place * 2 + grp) * res_rows
    half_rows = tokens // 2
    keys = 16 * res_rows
    queries = 16 * heads
    col = lax.broadcasted_iota(jnp.int32, (1, keys), 1)
    col_row = col // res_rows
    col_pos = base + col % res_rows
    same_row = (lax.broadcasted_iota(jnp.int32, (queries, keys), 0) % 16) == (
        lax.broadcasted_iota(jnp.int32, (queries, keys), 1) // res_rows
    )
    token = lax.broadcasted_iota(jnp.int32, (1, tokens), 1) - grp * half_rows
    token_bias = jnp.where((token >= 0) & (token < half_rows), 0.0, NEG_FILL)
    entry = lax.broadcasted_iota(jnp.int32, (queries, 128), 0)
    lane = lax.broadcasted_iota(jnp.int32, (queries, 128), 1)
    picks = [entry == (lane // 8) * 16 + side * 8 + lane % 8 for side in range(2)]

    def scores(g):
        lens = jnp.zeros((1, keys), jnp.int32)
        for r in range(16):
            lens = jnp.where(col_row == r, len_ref[16 * g + r], lens)
        live = jnp.where(col_pos < lens, 0.0, NEG_FILL)
        for copy in loads[g] + (new_loads if g == 0 else []):
            copy.wait()
        q = jnp.concatenate(
            [
                dq[16 * g : 16 * g + 16, h * HEAD_SIZE : (h + 1) * HEAD_SIZE]
                for h in range(heads)
            ],
            axis=0,
        )
        res_k = rk[16 * g : 16 * g + 16].reshape(keys, HEAD_SIZE)
        s1 = jnp.where(same_row, dot_t(q, res_k) * LOG2_SCALE + live, NEG_FILL)
        return s1, dot_t(q, nk[...]) * LOG2_SCALE + token_bias

    ahead = scores(0)
    for g in range(groups):
        s1, s2 = ahead
        if g + 1 < groups:
            ahead = scores(g + 1)
        res_v = rv[16 * g : 16 * g + 16].reshape(keys, HEAD_SIZE)
        top = jnp.maximum(jnp.max(s1, axis=1, keepdims=True), jnp.max(s2, axis=1, keepdims=True))
        top = top.astype(jnp.bfloat16).astype(jnp.float32)
        p1 = jnp.exp2(s1 - top).astype(jnp.bfloat16)
        p2 = jnp.exp2(s2 - top).astype(jnp.bfloat16)
        total = jnp.sum(p1.astype(jnp.float32), axis=1, keepdims=True) + jnp.sum(
            p2.astype(jnp.float32), axis=1, keepdims=True
        )
        values = (dot(p1, res_v) + dot(p2, nv[...])).reshape(heads, 2, 8, HEAD_SIZE)
        high = total.astype(jnp.bfloat16).astype(jnp.float32)
        for side in range(2):
            stats = [as_row(x, picks[side]) for x in (top, high, total - high)]
            stats = jnp.concatenate(stats + [jnp.zeros((13, 128), jnp.float32)], axis=0)
            at = side * groups + g
            out_ref[at, :128] = values[:, side].reshape(128, HEAD_SIZE).astype(jnp.bfloat16)
            out_ref[at, 128:] = stats.astype(jnp.bfloat16)


def factors_of(stats):
    top = stats[0][0:1]
    for part in stats[1:]:
        top = jnp.maximum(top, part[0:1])
    factors = [jnp.exp2(part[0:1] - top) for part in stats]
    total = factors[0] * (stats[0][1:2] + stats[0][2:3])
    for factor, part in zip(factors[1:], stats[1:]):
        total = total + factor * (part[1:2] + part[2:3])
    return factors, top, total


def pack_kernel(part_ref, nk_ref, nv_ref, out_ref):
    tokens = nk_ref.shape[0]
    count = part_ref.shape[0]

    half = tokens // 2
    for side in range(2):

        @pl.when(lax.axis_index("grp") == side)
        def _():
            out_ref[:half] = nk_ref[side * half : (side + 1) * half]
            out_ref[half:tokens] = nv_ref[side * half : (side + 1) * half]

    factors, top, total = factors_of(
        [part_ref[d, 128:].astype(jnp.float32) for d in range(count)]
    )
    columns = jnp.concatenate(factors, axis=0).T
    acc = jnp.zeros((128, HEAD_SIZE), jnp.float32)
    for d in range(count):
        acc = acc + part_ref[d, :128].astype(jnp.float32) * columns[:, d : d + 1]
    out_ref[tokens : tokens + 128] = acc.astype(jnp.bfloat16)
    high = total.astype(jnp.bfloat16).astype(jnp.float32)
    stats = [top, high, total - high, jnp.zeros((13, 128), jnp.float32)]
    out_ref[tokens + 128 :] = jnp.concatenate(stats, axis=0).astype(jnp.bfloat16)


def finish_kernel(all_ref, out_ref):
    count = all_ref.shape[0]
    begin = all_ref.shape[1] - 144
    for d in range(count):
        out_ref[begin * d : begin * (d + 1)] = all_ref[d, :begin]
    sides = []
    for side in range(2):
        parts = range(side, count, 2)
        factors, _, total = factors_of(
            [all_ref[d, begin + 128 :].astype(jnp.float32) for d in parts]
        )
        columns = jnp.concatenate([factor / total for factor in factors], axis=0)
        columns = columns.T
        acc = jnp.zeros((128, HEAD_SIZE), jnp.float32)
        for i, d in enumerate(parts):
            part = all_ref[d, begin : begin + 128].astype(jnp.float32)
            acc = acc + part * columns[:, i : i + 1]
        sides.append(acc.reshape(16, 8, HEAD_SIZE))
    value = jnp.stack(sides, axis=1).reshape(256, HEAD_SIZE).astype(jnp.bfloat16)
    out_ref[begin * count :] = value


def attend(where_ref, grp, own_ref, peer_ref, qs, acc, top):
    ctx, core, bound = where_ref[0], where_ref[1], where_ref[2]
    tokens = 96
    half = tokens // 2
    ring = own_ref.shape[0] // tokens
    blocks_per = min(8, ring)
    block = 2 * blocks_per * half
    row_block = 2 * tokens
    first = ctx * tokens
    q_pos = first + lax.broadcasted_iota(jnp.int32, (row_block, 1), 0) % tokens
    begin = jnp.where(q_pos < bound, 0, bound)
    col = lax.broadcasted_iota(jnp.int32, (1, block), 1)
    piece = col // half
    side = jnp.where(piece < blocks_per, core, 1 - core)
    key_pos0 = (2 * (piece % blocks_per) + side) * tokens + grp * half + col % half
    ones = jnp.ones((block, HEAD_SIZE), jnp.bfloat16)
    lowest = jnp.where(first < bound, 0, bound) // (2 * tokens)
    steps = (ctx // 2 - lowest) // blocks_per + 1

    def one(step, carry):
        low = lowest + step * blocks_per
        places = [
            pl.multiple_of(jnp.minimum(low + i, ring - 1) * tokens, PAGE_TOKENS)
            for i in range(blocks_per)
        ]
        k = jnp.concatenate(
            [ref[pl.ds(z, half), :] for ref in (own_ref, peer_ref) for z in places], axis=0
        )
        v = jnp.concatenate(
            [
                ref[pl.ds(pl.multiple_of(z + half, PAGE_TOKENS), half), :]
                for ref in (own_ref, peer_ref)
                for z in places
            ],
            axis=0,
        )
        v = jnp.concatenate([v, ones], axis=1)
        key_pos = key_pos0 + low * (2 * tokens)
        bias = jnp.where((key_pos <= q_pos) & (key_pos >= begin), 0.0, NEG_FILL)
        ahead = dot_t(qs[:row_block], k)
        for b in range(qs.shape[0] // row_block):
            rows_b = slice(b * row_block, (b + 1) * row_block)
            s = ahead * LOG2_SCALE + bias
            if b + 1 < qs.shape[0] // row_block:
                ahead = dot_t(qs[(b + 1) * row_block : (b + 2) * row_block], k)
            before = top[rows_b]
            after = jnp.maximum(before, jnp.max(s, axis=1, keepdims=True))
            p = jnp.exp2(s - after).astype(jnp.bfloat16)
            acc[rows_b] = acc[rows_b] * jnp.exp2(before - after) + dot(p, v)
            top[rows_b] = after
        return carry

    lax.fori_loop(0, steps, one, 0)


def first_kernel(where_ref, q_ref, own_ref, peer_ref, qs, acc, top):
    tokens = q_ref.shape[0]
    for h in range(q_ref.shape[1] // HEAD_SIZE):
        qs[h * tokens : (h + 1) * tokens] = q_ref[:, h * HEAD_SIZE : (h + 1) * HEAD_SIZE]
    acc[...] = jnp.zeros_like(acc)
    top[...] = jnp.full_like(top, NEG_FILL)
    attend(where_ref, where_ref[3], own_ref, peer_ref, qs, acc, top)


def second_kernel(
    where_ref, page_ref, a_own, a_peer, b_own, b_peer, qs, acc_in, top_in,
    out_ref, pk_ref, pv_ref, dec_ref, acc, top,
):
    ctx, core, grp = where_ref[0], where_ref[1], where_ref[3]
    tokens = out_ref.shape[0]
    heads = out_ref.shape[1] // HEAD_SIZE
    half = tokens // 2
    pages = tokens // PAGE_TOKENS
    for s in range(pk_ref.shape[0]):
        source = page_ref[s] // pages
        page = page_ref[s] - source * pages
        side = page // (pages // 2)
        row = (source // 2) * tokens + (page - side * (pages // 2)) * PAGE_TOKENS
        row = pl.multiple_of(row, PAGE_TOKENS)
        value_row = pl.multiple_of(row + half, PAGE_TOKENS)
        for same_side, same_core, ref in (
            (True, True, a_own), (True, False, a_peer), (False, True, b_own), (False, False, b_peer),
        ):
            there = ((side == grp) == same_side) & ((source % 2 == core) == same_core)

            @pl.when(there)
            def _():
                pk_ref[s] = ref[pl.ds(row, PAGE_TOKENS), :]
                pv_ref[s] = ref[pl.ds(value_row, PAGE_TOKENS), :]

    columns = dec_ref.shape[1] // HEAD_SIZE
    begin = a_own.shape[0] - 16 * columns
    for at_core, at_grp, ref in (
        (core, grp, a_own), (1 - core, grp, a_peer), (core, 1 - grp, b_own), (1 - core, 1 - grp, b_peer),
    ):
        row = pl.multiple_of((at_core * 2 + at_grp) * 16, 16)
        for h in range(columns):
            dec_ref[pl.ds(row, 16), h * HEAD_SIZE : (h + 1) * HEAD_SIZE] = ref[
                begin + 16 * h : begin + 16 * h + 16
            ]
    acc[...] = acc_in[...]
    top[...] = top_in[...]
    attend(where_ref, 1 - grp, b_own, b_peer, qs, acc, top)
    for h in range(heads):
        rows_h = slice(h * tokens, (h + 1) * tokens)
        out_ref[:, h * HEAD_SIZE : (h + 1) * HEAD_SIZE] = (
            acc[rows_h, :HEAD_SIZE] / acc[rows_h, HEAD_SIZE:]
        ).astype(jnp.bfloat16)


def local(
    new_queries,
    new_keys,
    new_values,
    segment_ids,
    page_table,
    decode_query_rows,
    resident_keys,
    resident_values,
    res_len,
):
    bf = jnp.bfloat16
    tokens = new_keys.shape[0]
    ring = lax.axis_size("far") * 2
    far, near, core, grp = (lax.axis_index(a) for a in ("far", "near", "core", "grp"))
    ctx = (far * 2 + near) * 2 + core
    rows, width = decode_query_rows.shape
    queries = 16 * (width // HEAD_SIZE)
    res_rows = resident_keys.shape[1]
    pages = tokens // PAGE_TOKENS
    i32 = jnp.int32

    groups = rows // 16
    part = pl.pallas_call(
        partial_kernel,
        out_shape=jax.ShapeDtypeStruct((2 * groups, 144, HEAD_SIZE), bf),
        in_specs=[SMEM] + [HBM] * 5,
        out_specs=VMEM,
        scratch_shapes=[
            pltpu.VMEM(decode_query_rows.shape, bf),
            pltpu.VMEM(resident_keys.shape, bf),
            pltpu.VMEM(resident_values.shape, bf),
            pltpu.VMEM(new_keys.shape, bf),
            pltpu.VMEM(new_values.shape, bf),
            pltpu.SemaphoreType.DMA((3 * groups + 2,)),
        ],
        compiler_params=pltpu.CompilerParams(vmem_limit_bytes=63 * 1024 * 1024),
    )(res_len, decode_query_rows, resident_keys, resident_values, new_keys, new_values)
    bound = jnp.sum((segment_ids == 0).astype(i32))
    slots = ctx * pages + jnp.arange(pages, dtype=i32)
    ids = jnp.arange(page_table.shape[0], dtype=i32)
    page_from = jnp.sum(jnp.where(page_table[None, :] == slots[:, None], ids[None, :], 0), axis=1)
    where_b = jnp.stack([ctx, core, bound, grp]).astype(i32)
    part = lax.all_to_all(part, ("near", "core", "grp"), 0, 0, tiled=True)
    part, where_b, page_from = lax.optimization_barrier((part, where_b, page_from))
    packed = pl.pallas_call(
        pack_kernel,
        out_shape=jax.ShapeDtypeStruct((tokens + 144, HEAD_SIZE), bf),
        in_specs=[VMEM] * 3,
        out_specs=VMEM,
        compiler_params=PARAMS,
    )(part, new_keys, new_values)
    gathered = lax.all_gather(packed, ("far", "near"), axis=0)
    swap = [(0, 1), (1, 0)]
    a_own = pl.pallas_call(
        finish_kernel,
        out_shape=jax.ShapeDtypeStruct((ring * tokens + queries, HEAD_SIZE), bf),
        in_specs=[VMEM],
        out_specs=VMEM,
        compiler_params=PARAMS,
    )(gathered)
    b_own = lax.ppermute(a_own, "grp", swap)
    a_peer = lax.ppermute(a_own, "core", swap)
    b_peer = lax.ppermute(b_own, "core", swap)
    stacked = tokens * (new_queries.shape[1] // HEAD_SIZE)
    state = pl.pallas_call(
        first_kernel,
        out_shape=(
            jax.ShapeDtypeStruct((stacked, HEAD_SIZE), bf),
            jax.ShapeDtypeStruct((stacked, 2 * HEAD_SIZE), jnp.float32),
            jax.ShapeDtypeStruct((stacked, 1), jnp.float32),
        ),
        in_specs=[SMEM] + [VMEM] * 3,
        out_specs=(VMEM,) * 3,
        compiler_params=PARAMS,
    )(where_b, new_queries, a_own, a_peer)
    prefill_out, paged_keys, paged_values, decode_out = pl.pallas_call(
        second_kernel,
        out_shape=(
            jax.ShapeDtypeStruct(new_queries.shape, bf),
            jax.ShapeDtypeStruct((pages, PAGE_TOKENS, HEAD_SIZE), bf),
            jax.ShapeDtypeStruct((pages, PAGE_TOKENS, HEAD_SIZE), bf),
            jax.ShapeDtypeStruct((rows, width), bf),
        ),
        in_specs=[SMEM, SMEM] + [VMEM] * 7,
        out_specs=(VMEM,) * 4,
        scratch_shapes=[
            pltpu.VMEM((stacked, 2 * HEAD_SIZE), jnp.float32),
            pltpu.VMEM((stacked, 1), jnp.float32),
        ],
        compiler_params=PARAMS,
    )(where_b, page_from, a_own, a_peer, b_own, b_peer, *state)
    return (prefill_out, paged_keys, paged_values, decode_out)


def solution(mesh):
    sizes = mesh.shape
    fine = Mesh(
        np.asarray(mesh.devices).reshape(
            sizes["ctx"] // 4, 2, 2, sizes["head"], sizes["grp"]
        ),
        ("far", "near", "core", "head", "grp"),
    )
    ctx = ("far", "near", "core")
    return jax.shard_map(
        local,
        mesh=fine,
        in_specs=(
            P(ctx, ("head", "grp")),
            P(ctx, "head"),
            P(ctx, "head"),
            P(),
            P(),
            P(None, "head"),
            P(None, ctx + ("grp",), "head"),
            P(None, ctx + ("grp",), "head"),
            P(),
        ),
        out_specs=(
            P(ctx, ("head", "grp")),
            P(ctx, None, "head"),
            P(ctx, None, "head"),
            P(None, "head"),
        ),
        check_vma=False,
    )
```

```python
import jax
import jax.numpy as jnp
import numpy as np
from jax import lax
from jax.experimental import pallas as pl
from jax.experimental.pallas import tpu as pltpu
from jax.sharding import Mesh, PartitionSpec as P

HEAD_SIZE = 128
PAGE_TOKENS = 16
NEG_FILL = -1e30
LOG2_SCALE = HEAD_SIZE**-0.5 * 1.4426950408889634
VMEM = pl.BlockSpec(memory_space=pltpu.VMEM)
HBM = pl.BlockSpec(memory_space=pltpu.HBM)
SMEM = pl.BlockSpec(memory_space=pltpu.SMEM)
PARAMS = pltpu.CompilerParams(vmem_limit_bytes=48 * 1024 * 1024)


def dot_t(a, b):
    return lax.dot_general(a, b, (((1,), (1,)), ((), ())), preferred_element_type=jnp.float32)


def dot(a, b):
    return jnp.dot(a, b, preferred_element_type=jnp.float32)


def as_row(column, pick):
    return jnp.sum(jnp.where(pick, column, 0.0), axis=0, keepdims=True)


def partial_kernel(
    len_ref, dq_hbm, rk_hbm, rv_hbm, nk_hbm, nv_hbm, out_ref, dq, rk, rv, nk, nv, sems
):
    groups = dq.shape[0] // 16
    res_rows = rk.shape[1]
    heads = dq.shape[1] // HEAD_SIZE
    tokens = nk.shape[0]
    loads = []
    for g in range(groups):
        rows = pl.ds(16 * g, 16)
        loads.append(
            [
                pltpu.make_async_copy(src.at[rows], dst.at[rows], sems.at[3 * g + i])
                for i, (src, dst) in enumerate(((dq_hbm, dq), (rk_hbm, rk), (rv_hbm, rv)))
            ]
        )
    new_loads = [
        pltpu.make_async_copy(src, dst, sems.at[3 * groups + i])
        for i, (src, dst) in enumerate(((nk_hbm, nk), (nv_hbm, nv)))
    ]
    for copy in loads[0] + new_loads + [copy for group in loads[1:] for copy in group]:
        copy.start()
    grp = lax.axis_index("grp")
    place = (lax.axis_index("far") * 2 + lax.axis_index("near")) * 2 + lax.axis_index("core")
    base = (place * 2 + grp) * res_rows
    half_rows = tokens // 2
    keys = 16 * res_rows
    queries = 16 * heads
    col = lax.broadcasted_iota(jnp.int32, (1, keys), 1)
    col_row = col // res_rows
    col_pos = base + col % res_rows
    same_row = (lax.broadcasted_iota(jnp.int32, (queries, keys), 0) % 16) == (
        lax.broadcasted_iota(jnp.int32, (queries, keys), 1) // res_rows
    )
    token = lax.broadcasted_iota(jnp.int32, (1, tokens), 1) - grp * half_rows
    token_bias = jnp.where((token >= 0) & (token < half_rows), 0.0, NEG_FILL)
    entry = lax.broadcasted_iota(jnp.int32, (queries, 128), 0)
    lane = lax.broadcasted_iota(jnp.int32, (queries, 128), 1)
    picks = [entry == (lane // 8) * 16 + side * 8 + lane % 8 for side in range(2)]

    def scores(g):
        lens = jnp.zeros((1, keys), jnp.int32)
        for r in range(16):
            lens = jnp.where(col_row == r, len_ref[16 * g + r], lens)
        live = jnp.where(col_pos < lens, 0.0, NEG_FILL)
        for copy in loads[g] + (new_loads if g == 0 else []):
            copy.wait()
        q = jnp.concatenate(
            [
                dq[16 * g : 16 * g + 16, h * HEAD_SIZE : (h + 1) * HEAD_SIZE]
                for h in range(heads)
            ],
            axis=0,
        )
        res_k = rk[16 * g : 16 * g + 16].reshape(keys, HEAD_SIZE)
        s1 = jnp.where(same_row, dot_t(q, res_k) * LOG2_SCALE + live, NEG_FILL)
        return s1, dot_t(q, nk[...]) * LOG2_SCALE + token_bias

    ahead = scores(0)
    for g in range(groups):
        s1, s2 = ahead
        if g + 1 < groups:
            ahead = scores(g + 1)
        res_v = rv[16 * g : 16 * g + 16].reshape(keys, HEAD_SIZE)
        top = jnp.maximum(jnp.max(s1, axis=1, keepdims=True), jnp.max(s2, axis=1, keepdims=True))
        top = top.astype(jnp.bfloat16).astype(jnp.float32)
        p1 = jnp.exp2(s1 - top).astype(jnp.bfloat16)
        p2 = jnp.exp2(s2 - top).astype(jnp.bfloat16)
        total = jnp.sum(p1.astype(jnp.float32), axis=1, keepdims=True) + jnp.sum(
            p2.astype(jnp.float32), axis=1, keepdims=True
        )
        values = (dot(p1, res_v) + dot(p2, nv[...])).reshape(heads, 2, 8, HEAD_SIZE)
        high = total.astype(jnp.bfloat16).astype(jnp.float32)
        for side in range(2):
            stats = [as_row(x, picks[side]) for x in (top, high, total - high)]
            stats = jnp.concatenate(stats + [jnp.zeros((13, 128), jnp.float32)], axis=0)
            at = side * groups + g
            out_ref[at, :128] = values[:, side].reshape(128, HEAD_SIZE).astype(jnp.bfloat16)
            out_ref[at, 128:] = stats.astype(jnp.bfloat16)


def factors_of(stats):
    top = stats[0][0:1]
    for part in stats[1:]:
        top = jnp.maximum(top, part[0:1])
    factors = [jnp.exp2(part[0:1] - top) for part in stats]
    total = factors[0] * (stats[0][1:2] + stats[0][2:3])
    for factor, part in zip(factors[1:], stats[1:]):
        total = total + factor * (part[1:2] + part[2:3])
    return factors, top, total


def pack_kernel(part_ref, nk_ref, nv_ref, out_ref):
    tokens = nk_ref.shape[0]
    count = part_ref.shape[0]

    half = tokens // 2
    for side in range(2):

        @pl.when(lax.axis_index("grp") == side)
        def _():
            out_ref[:half] = nk_ref[side * half : (side + 1) * half]
            out_ref[half:tokens] = nv_ref[side * half : (side + 1) * half]

    factors, top, total = factors_of(
        [part_ref[d, 128:].astype(jnp.float32) for d in range(count)]
    )
    columns = jnp.concatenate(factors, axis=0).T
    acc = jnp.zeros((128, HEAD_SIZE), jnp.float32)
    for d in range(count):
        acc = acc + part_ref[d, :128].astype(jnp.float32) * columns[:, d : d + 1]
    out_ref[tokens : tokens + 128] = acc.astype(jnp.bfloat16)
    high = total.astype(jnp.bfloat16).astype(jnp.float32)
    stats = [top, high, total - high, jnp.zeros((13, 128), jnp.float32)]
    out_ref[tokens + 128 :] = jnp.concatenate(stats, axis=0).astype(jnp.bfloat16)


def finish_kernel(all_ref, out_ref):
    count = all_ref.shape[0]
    begin = all_ref.shape[1] - 144
    for d in range(count):
        out_ref[begin * d : begin * (d + 1)] = all_ref[d, :begin]
    sides = []
    for side in range(2):
        parts = range(side, count, 2)
        factors, _, total = factors_of(
            [all_ref[d, begin + 128 :].astype(jnp.float32) for d in parts]
        )
        columns = jnp.concatenate([factor / total for factor in factors], axis=0)
        columns = columns.T
        acc = jnp.zeros((128, HEAD_SIZE), jnp.float32)
        for i, d in enumerate(parts):
            part = all_ref[d, begin : begin + 128].astype(jnp.float32)
            acc = acc + part * columns[:, i : i + 1]
        sides.append(acc.reshape(16, 8, HEAD_SIZE))
    value = jnp.stack(sides, axis=1).reshape(256, HEAD_SIZE).astype(jnp.bfloat16)
    out_ref[begin * count :] = value


def attend(where_ref, grp, own_ref, peer_ref, qs, acc, top):
    ctx, core, bound = where_ref[0], where_ref[1], where_ref[2]
    tokens = 96
    half = tokens // 2
    ring = own_ref.shape[0] // tokens
    blocks_per = min(8, ring)
    block = 2 * blocks_per * half
    row_block = 2 * tokens
    first = ctx * tokens
    q_pos = first + lax.broadcasted_iota(jnp.int32, (row_block, 1), 0) % tokens
    begin = jnp.where(q_pos < bound, 0, bound)
    col = lax.broadcasted_iota(jnp.int32, (1, block), 1)
    piece = col // half
    side = jnp.where(piece < blocks_per, core, 1 - core)
    key_pos0 = (2 * (piece % blocks_per) + side) * tokens + grp * half + col % half
    ones = jnp.ones((block, HEAD_SIZE), jnp.bfloat16)
    lowest = jnp.where(first < bound, 0, bound) // (2 * tokens)
    steps = (ctx // 2 - lowest) // blocks_per + 1

    def one(step, carry):
        low = lowest + step * blocks_per
        places = [
            pl.multiple_of(jnp.minimum(low + i, ring - 1) * tokens, PAGE_TOKENS)
            for i in range(blocks_per)
        ]
        k = jnp.concatenate(
            [ref[pl.ds(z, half), :] for ref in (own_ref, peer_ref) for z in places], axis=0
        )
        v = jnp.concatenate(
            [
                ref[pl.ds(pl.multiple_of(z + half, PAGE_TOKENS), half), :]
                for ref in (own_ref, peer_ref)
                for z in places
            ],
            axis=0,
        )
        v = jnp.concatenate([v, ones], axis=1)
        key_pos = key_pos0 + low * (2 * tokens)
        bias = jnp.where((key_pos <= q_pos) & (key_pos >= begin), 0.0, NEG_FILL)
        ahead = dot_t(qs[:row_block], k)
        for b in range(qs.shape[0] // row_block):
            rows_b = slice(b * row_block, (b + 1) * row_block)
            s = ahead * LOG2_SCALE + bias
            if b + 1 < qs.shape[0] // row_block:
                ahead = dot_t(qs[(b + 1) * row_block : (b + 2) * row_block], k)
            before = top[rows_b]
            after = jnp.maximum(before, jnp.max(s, axis=1, keepdims=True))
            p = jnp.exp2(s - after).astype(jnp.bfloat16)
            acc[rows_b] = acc[rows_b] * jnp.exp2(before - after) + dot(p, v)
            top[rows_b] = after
        return carry

    lax.fori_loop(0, steps, one, 0)


def first_kernel(where_ref, q_ref, own_ref, peer_ref, qs, acc, top):
    tokens = q_ref.shape[0]
    for h in range(q_ref.shape[1] // HEAD_SIZE):
        qs[h * tokens : (h + 1) * tokens] = q_ref[:, h * HEAD_SIZE : (h + 1) * HEAD_SIZE]
    acc[...] = jnp.zeros_like(acc)
    top[...] = jnp.full_like(top, NEG_FILL)
    attend(where_ref, where_ref[3], own_ref, peer_ref, qs, acc, top)


def second_kernel(
    where_ref, page_ref, a_own, a_peer, b_own, b_peer, qs, acc_in, top_in,
    out_ref, pk_ref, pv_ref, dec_ref, acc, top,
):
    ctx, core, grp = where_ref[0], where_ref[1], where_ref[3]
    tokens = out_ref.shape[0]
    heads = out_ref.shape[1] // HEAD_SIZE
    half = tokens // 2
    pages = tokens // PAGE_TOKENS
    for s in range(pk_ref.shape[0]):
        source = page_ref[s] // pages
        page = page_ref[s] - source * pages
        side = page // (pages // 2)
        row = (source // 2) * tokens + (page - side * (pages // 2)) * PAGE_TOKENS
        row = pl.multiple_of(row, PAGE_TOKENS)
        value_row = pl.multiple_of(row + half, PAGE_TOKENS)
        own_side = side == grp
        own_core = source % 2 == core
        for out, at in ((pk_ref, row), (pv_ref, value_row)):
            a = jnp.where(own_core, a_own[pl.ds(at, PAGE_TOKENS), :], a_peer[pl.ds(at, PAGE_TOKENS), :])
            b = jnp.where(own_core, b_own[pl.ds(at, PAGE_TOKENS), :], b_peer[pl.ds(at, PAGE_TOKENS), :])
            out[s] = jnp.where(own_side, a, b)

    columns = dec_ref.shape[1] // HEAD_SIZE
    begin = a_own.shape[0] - 16 * columns
    for at_core, at_grp, ref in (
        (core, grp, a_own), (1 - core, grp, a_peer), (core, 1 - grp, b_own), (1 - core, 1 - grp, b_peer),
    ):
        row = pl.multiple_of((at_core * 2 + at_grp) * 16, 16)
        for h in range(columns):
            dec_ref[pl.ds(row, 16), h * HEAD_SIZE : (h + 1) * HEAD_SIZE] = ref[
                begin + 16 * h : begin + 16 * h + 16
            ]
    acc[...] = acc_in[...]
    top[...] = top_in[...]
    attend(where_ref, 1 - grp, b_own, b_peer, qs, acc, top)
    for h in range(heads):
        rows_h = slice(h * tokens, (h + 1) * tokens)
        out_ref[:, h * HEAD_SIZE : (h + 1) * HEAD_SIZE] = (
            acc[rows_h, :HEAD_SIZE] / acc[rows_h, HEAD_SIZE:]
        ).astype(jnp.bfloat16)


def local(
    new_queries,
    new_keys,
    new_values,
    segment_ids,
    page_table,
    decode_query_rows,
    resident_keys,
    resident_values,
    res_len,
):
    bf = jnp.bfloat16
    tokens = new_keys.shape[0]
    ring = lax.axis_size("far") * 2
    far, near, core, grp = (lax.axis_index(a) for a in ("far", "near", "core", "grp"))
    ctx = (far * 2 + near) * 2 + core
    rows, width = decode_query_rows.shape
    queries = 16 * (width // HEAD_SIZE)
    res_rows = resident_keys.shape[1]
    pages = tokens // PAGE_TOKENS
    i32 = jnp.int32

    groups = rows // 16
    part = pl.pallas_call(
        partial_kernel,
        out_shape=jax.ShapeDtypeStruct((2 * groups, 144, HEAD_SIZE), bf),
        in_specs=[SMEM] + [HBM] * 5,
        out_specs=VMEM,
        scratch_shapes=[
            pltpu.VMEM(decode_query_rows.shape, bf),
            pltpu.VMEM(resident_keys.shape, bf),
            pltpu.VMEM(resident_values.shape, bf),
            pltpu.VMEM(new_keys.shape, bf),
            pltpu.VMEM(new_values.shape, bf),
            pltpu.SemaphoreType.DMA((3 * groups + 2,)),
        ],
        compiler_params=pltpu.CompilerParams(vmem_limit_bytes=63 * 1024 * 1024),
    )(res_len, decode_query_rows, resident_keys, resident_values, new_keys, new_values)
    bound = jnp.sum((segment_ids == 0).astype(i32))
    slots = ctx * pages + jnp.arange(pages, dtype=i32)
    ids = jnp.arange(page_table.shape[0], dtype=i32)
    page_from = jnp.sum(jnp.where(page_table[None, :] == slots[:, None], ids[None, :], 0), axis=1)
    where_b = jnp.stack([ctx, core, bound, grp]).astype(i32)
    part = lax.all_to_all(part, ("near", "core", "grp"), 0, 0, tiled=True)
    part, where_b, page_from = lax.optimization_barrier((part, where_b, page_from))
    packed = pl.pallas_call(
        pack_kernel,
        out_shape=jax.ShapeDtypeStruct((tokens + 144, HEAD_SIZE), bf),
        in_specs=[VMEM] * 3,
        out_specs=VMEM,
        compiler_params=PARAMS,
    )(part, new_keys, new_values)
    gathered = lax.all_gather(packed, ("far", "near"), axis=0)
    swap = [(0, 1), (1, 0)]
    a_own = pl.pallas_call(
        finish_kernel,
        out_shape=jax.ShapeDtypeStruct((ring * tokens + queries, HEAD_SIZE), bf),
        in_specs=[VMEM],
        out_specs=VMEM,
        compiler_params=PARAMS,
    )(gathered)
    b_own = lax.ppermute(a_own, "grp", swap)
    a_peer = lax.ppermute(a_own, "core", swap)
    b_peer = lax.ppermute(b_own, "core", swap)
    stacked = tokens * (new_queries.shape[1] // HEAD_SIZE)
    state = pl.pallas_call(
        first_kernel,
        out_shape=(
            jax.ShapeDtypeStruct((stacked, HEAD_SIZE), bf),
            jax.ShapeDtypeStruct((stacked, 2 * HEAD_SIZE), jnp.float32),
            jax.ShapeDtypeStruct((stacked, 1), jnp.float32),
        ),
        in_specs=[SMEM] + [VMEM] * 3,
        out_specs=(VMEM,) * 3,
        compiler_params=PARAMS,
    )(where_b, new_queries, a_own, a_peer)
    prefill_out, paged_keys, paged_values, decode_out = pl.pallas_call(
        second_kernel,
        out_shape=(
            jax.ShapeDtypeStruct(new_queries.shape, bf),
            jax.ShapeDtypeStruct((pages, PAGE_TOKENS, HEAD_SIZE), bf),
            jax.ShapeDtypeStruct((pages, PAGE_TOKENS, HEAD_SIZE), bf),
            jax.ShapeDtypeStruct((rows, width), bf),
        ),
        in_specs=[SMEM, SMEM] + [VMEM] * 7,
        out_specs=(VMEM,) * 4,
        scratch_shapes=[
            pltpu.VMEM((stacked, 2 * HEAD_SIZE), jnp.float32),
            pltpu.VMEM((stacked, 1), jnp.float32),
        ],
        compiler_params=PARAMS,
    )(where_b, page_from, a_own, a_peer, b_own, b_peer, *state)
    return (prefill_out, paged_keys, paged_values, decode_out)


def solution(mesh):
    sizes = mesh.shape
    fine = Mesh(
        np.asarray(mesh.devices).reshape(
            sizes["ctx"] // 4, 2, 2, sizes["head"], sizes["grp"]
        ),
        ("far", "near", "core", "head", "grp"),
    )
    ctx = ("far", "near", "core")
    return jax.shard_map(
        local,
        mesh=fine,
        in_specs=(
            P(ctx, ("head", "grp")),
            P(ctx, "head"),
            P(ctx, "head"),
            P(),
            P(),
            P(None, "head"),
            P(None, ctx + ("grp",), "head"),
            P(None, ctx + ("grp",), "head"),
            P(),
        ),
        out_specs=(
            P(ctx, ("head", "grp")),
            P(ctx, None, "head"),
            P(ctx, None, "head"),
            P(None, "head"),
        ),
        check_vma=False,
    )
```
